512 devices in a mesh: dp: 16 (over x_lo, y), expert: 32 (over z, x_hi, core).
Axes of the slice: x: 4 (x_hi: 2, x_lo: 2; x = x_hi * 2 + x_lo), y: 8, z: 8, core: 2. Of those that a mesh axis runs over, the one named last changes fastest.
Arguments:
- tokens: bfloat16 [65536, 1024], P(('dp', 'expert')), may hold values from -6 to 6
- cotangent: bfloat16 [65536, 1024], P(('dp', 'expert')), may hold values from -6 to 6
- gates: float32 [65536, 4], P(('dp', 'expert')), may hold values from 0.05 to 0.5
- expert_ids: int32 [65536, 4], P(('dp', 'expert')), may hold values from 0 to 31, all different within a row; in each aligned block of 128 rows (0 to 127, 128 to 255, ...) at most 24 rows name the same one
- placement: int32 [32], replicated, may hold values from 0 to 31, each once
- partner: int32 [32], replicated, may hold values from 0 to 31, as said below
- w_gate_up: bfloat16 [32, 1024, 1024], P('expert', 'dp'), may hold values from -0.1875 to 0.1875
- w_down: bfloat16 [32, 512, 1024], P('expert', 'dp'), may hold values from -0.25 to 0.25
Outputs:
- token_grad: bfloat16 [65536, 1024], P(('dp', 'expert'))
- grad_gate_up: float32 [32, 1024, 1024], P('expert', 'dp')
- grad_down: float32 [32, 512, 1024], P('expert', 'dp')
The draws below stay inside these ranges and needn't reach their ends.
Inputs may be any that keep to these rules, and one draw needn't show every extreme that they name: `expert_ids`: within each device's aligned block of 128 rows no expert is named by more than 24 choices; the 4 entries of a row differ. `placement`: each index appears once. partner[partner[j]] = j, and partner[j] is j or differs from j in exactly one bit of its binary form.
All inputs are finite; a program needn't handle non-finite values.
Results may differ from the reference program's by a relative error of at most 0.02.
Values may be sent and summed in bfloat16 or wider, within the bound.
A program may use at most 64 MiB of HBM per device.

```python
import math
import jax
import jax.numpy as jnp
import numpy as np
from jax import lax

D = 1024
FF = 512
TOPK = 4
TOK_DEV = 128
EXPERTS = 32
TOKENS = 65536
CAP = 24
N_DP = 16
N_EXPERT = 32


def draw_partner(key, part):
    key = jax.random.fold_in(key, 11)
    levels = EXPERTS.bit_length() - 1
    index = jnp.arange(EXPERTS, dtype=jnp.int32)
    bit_order = jax.random.permutation(jax.random.fold_in(key, 1), levels).astype(jnp.int32)
    result = index
    unmatched = jnp.ones((EXPERTS,), bool)
    for level in range(levels):
        mask = jnp.left_shift(jnp.int32(1), bit_order[level])
        mate = jnp.bitwise_xor(index, mask)
        lower = jnp.minimum(index, mate)
        coin = jax.random.randint(jax.random.fold_in(key, 100 + level), (EXPERTS,), 0, 2).astype(jnp.int32)
        paired = unmatched & unmatched[mate] & (coin[lower] == 1)
        result = jnp.where(paired, mate, result)
        unmatched = unmatched & jnp.logical_not(paired)
    return result.astype(jnp.int32)


def shard_levels(key, dims, split, low, top_value):
    def one(axis_at, parts):
        draws = jax.random.uniform(jax.random.fold_in(jax.random.fold_in(key, 6), axis_at), (parts,), jnp.float32, low / len(split), top_value / len(split))
        return jnp.repeat(jnp.exp(draws), dims[axis_at] // parts).reshape((-1,) + (1,) * (len(dims) - axis_at - 1))

    loudness = one(*split[0])
    for cut in split[1:]:
        loudness = loudness * one(*cut)
    return loudness


def deal_out(own_key, own, number, rows, amount, top, reach, lean):
    sequence = jax.random.permutation(own_key, amount)
    crowded, ordinary = portions_of(amount, rows * top, reach, lean, True), portions_of(amount, rows * top, reach, lean, False)
    places = jnp.arange(amount)

    def named(sizes, rotation):
        used = int((sizes > 0).sum())
        fixed = max(1, used // 4)
        moved = fixed + (places - fixed + rotation * (used - fixed)) % max(1, amount - fixed)
        return jnp.zeros((amount,), jnp.int32).at[sequence[jnp.where(places < fixed, places, moved)]].set(jnp.asarray(sizes, jnp.int32))

    sizes = jnp.where(number % 4 == 0, named(crowded, number // 4), named(ordinary, number - number // 4 - 1))
    mixed = jax.random.permutation(jax.random.fold_in(own, 3), amount)
    source_of, sink = mixed[0:amount // 2 * 2:2], mixed[1:amount // 2 * 2:2]
    room = jnp.minimum(sizes[source_of] - 1, reach - sizes[sink]) // 2
    room = jnp.where((source_of == sequence[0]) | (sink == sequence[0]) | (sizes[sink] == 0), 0, jnp.maximum(room, 0))
    moved = jax.random.randint(jax.random.fold_in(own, 4), (amount // 2,), 0, 1 << 20) % (room + 1)
    sizes = sizes.at[source_of].add(-moved).at[sink].add(moved)
    items = jnp.searchsorted(jnp.cumsum(sizes), jnp.arange(rows * top), side="right").astype(jnp.int32)
    listing = items.reshape(top, rows).T
    listing = listing[jax.random.permutation(jax.random.fold_in(own, 1), rows)]
    rotation = jax.random.randint(jax.random.fold_in(own, 2), (rows, 1), 0, top)
    return jnp.take_along_axis(listing, (jnp.arange(top)[None, :] + rotation) % top, axis=1)


def portions_of(number_of, total, most, lean, full):
    weights = [(1 << 20) // math.isqrt(grade ** lean) + 1 for grade in range(1, number_of + 1)]
    largest = most if full else min(most, max(-(-total // number_of), total * weights[0] // sum(weights)))
    least = 1 if total - largest >= number_of - 1 else 0
    given, surplus = [largest] + [least] * (number_of - 1), total - largest - least * (number_of - 1)
    while surplus > 0:
        candidates = [i for i in range(1, number_of) if given[i] < largest] or [i for i in range(1, number_of) if given[i] < most]
        pool, budget = sum([weights[i] for i in candidates]), surplus
        for i in candidates:
            addition = min(most - given[i], max(1, budget * weights[i] // pool), surplus)
            given[i] = given[i] + addition
            surplus = surplus - addition
    return np.array(given)


def bell_draw(key, dims, width, bound, cuts=(), kind=jnp.bfloat16):
    array = jax.random.normal(key, dims, jnp.float32) * width
    if len(cuts) > 0:
        array = shard_levels(key, dims, cuts, -0.22, 0.18) * array
    return jnp.clip(array, min=-bound, max=bound).astype(kind)


def setup_inputs(seed: int = 0) -> dict:
    arg_keys = jax.random.split(jax.random.key(seed), 9)
    tokens = bell_draw(arg_keys[0], (TOKENS, D), 1.0, 6.0, ((0, 512),))
    cotangent = bell_draw(arg_keys[1], (TOKENS, D), 1.0, 6.0, ((0, 512),))
    gates = jnp.clip(jnp.exp(math.log(0.5) - 2.3025851 * jax.random.uniform(arg_keys[2], (TOKENS, TOPK), jnp.float32) ** shard_levels(arg_keys[2], (TOKENS, TOPK), ((0, 512),), -0.2, 0.2)), 0.05, 0.5)
    expert_ids_keys = jax.random.split(jax.random.fold_in(arg_keys[3], 1), TOKENS // TOK_DEV)
    expert_ids_turns = jax.random.permutation(jax.random.fold_in(arg_keys[3], 3), TOKENS // TOK_DEV)
    expert_ids = jax.vmap(lambda own, number: deal_out(jax.random.fold_in(arg_keys[3], 2), own, number, TOK_DEV, EXPERTS, TOPK, CAP, 2))(expert_ids_keys, expert_ids_turns).reshape((TOKENS, TOPK))
    placement = jax.random.permutation(arg_keys[4], EXPERTS).astype(jnp.int32)
    partner = draw_partner(jax.random.fold_in(arg_keys[8], 71), 0)
    w_gate_up = bell_draw(arg_keys[6], (EXPERTS, D, 2 * FF), D ** -0.5, 0.1875, ((0, 32), (1, 16)))
    w_down = bell_draw(arg_keys[7], (EXPERTS, FF, D), FF ** -0.5, 0.25, ((0, 32), (1, 16)))
    return {"tokens": tokens, "cotangent": cotangent, "gates": gates, "expert_ids": expert_ids, "placement": placement, "partner": partner, "w_gate_up": w_gate_up, "w_down": w_down}


def expert_pass(inputs, upstream, weight_gu, weight_dn):
    hidden_units = weight_dn.shape[0]
    pre = jnp.dot(inputs, weight_gu, preferred_element_type=jnp.float32)
    gate_pre = pre[:, :hidden_units]
    up_pre = pre[:, hidden_units:]
    sigma = jax.nn.sigmoid(gate_pre)
    active = gate_pre * sigma
    hidden = (active * up_pre).astype(jnp.bfloat16)
    grad_hidden = lax.dot_general(upstream, weight_dn, (((1,), (1,)), ((), ())), preferred_element_type=jnp.float32)
    grad_gate = grad_hidden * up_pre * (sigma * (1.0 + gate_pre * (1.0 - sigma)))
    grad_up = grad_hidden * active
    joined = jnp.concatenate([grad_gate, grad_up], axis=1).astype(jnp.bfloat16)
    back = lax.dot_general(joined, weight_gu, (((1,), (1,)), ((), ())), preferred_element_type=jnp.float32).astype(jnp.bfloat16)
    part_gu = lax.dot_general(inputs, joined, (((0,), (0,)), ((), ())), preferred_element_type=jnp.float32)
    part_dn = lax.dot_general(hidden, upstream, (((0,), (0,)), ((), ())), preferred_element_type=jnp.float32)
    return back, part_gu, part_dn


def reference(tokens, cotangent, gates, expert_ids, placement, partner, w_gate_up, w_down):
    entries = TOKENS * TOPK
    per_group = entries // N_DP
    block_rows = N_EXPERT * CAP
    flat_ids = expert_ids.reshape(entries).astype(jnp.int32)
    group = jnp.arange(entries, dtype=jnp.int32) // per_group
    sort_key = (flat_ids * N_DP + group).astype(jnp.int32)
    order = jnp.argsort(sort_key, stable=True).astype(jnp.int32)
    counts = jnp.zeros((EXPERTS * N_DP,), jnp.int32).at[sort_key].add(1)
    starts = (jnp.cumsum(counts) - counts).astype(jnp.int32)
    padded = jnp.concatenate([order, jnp.zeros((block_rows,), jnp.int32)])
    flat_gates = gates.reshape(entries)

    def step(carry, pair):
        token_acc, gu_acc, dn_acc = carry
        expert = pair // N_DP
        chosen = lax.dynamic_slice_in_dim(padded, starts[pair], block_rows)
        live = jnp.arange(block_rows, dtype=jnp.int32) < counts[pair]
        rows = (chosen // TOPK).astype(jnp.int32)
        inputs = jnp.where(live[:, None], tokens[rows], jnp.zeros((), tokens.dtype))
        scaled = (flat_gates[chosen][:, None] * cotangent[rows].astype(jnp.float32)).astype(jnp.bfloat16)
        upstream = jnp.where(live[:, None], scaled, jnp.zeros((), scaled.dtype))
        target = placement[expert]
        holder = partner[target]
        back, part_gu, part_dn = expert_pass(inputs, upstream, w_gate_up[holder], w_down[holder])
        back_wide = lax.optimization_barrier(back).astype(jnp.float32)
        token_acc = token_acc.at[rows].add(jnp.where(live[:, None], back_wide, jnp.zeros((), jnp.float32)))
        narrow_gu = lax.optimization_barrier(part_gu.astype(jnp.bfloat16)).astype(jnp.float32)
        narrow_dn = lax.optimization_barrier(part_dn.astype(jnp.bfloat16)).astype(jnp.float32)
        gu_acc = gu_acc.at[target].add(narrow_gu)
        dn_acc = dn_acc.at[target].add(narrow_dn)
        return (token_acc, gu_acc, dn_acc), None

    start = (jnp.zeros((TOKENS, D), jnp.float32), jnp.zeros((EXPERTS, D, 2 * FF), jnp.float32), jnp.zeros((EXPERTS, FF, D), jnp.float32))
    final, _ = lax.scan(step, start, jnp.arange(EXPERTS * N_DP, dtype=jnp.int32))
    token_acc, gu_acc, dn_acc = final
    return token_acc.astype(jnp.bfloat16), gu_acc, dn_acc
```

```python
import functools

import jax
import jax.numpy as jnp
from jax import lax
from jax.experimental import pallas as pl
from jax.experimental.pallas import tpu as pltpu
from jax.sharding import PartitionSpec as P

MESH = pl.DeviceIdType.MESH
BF16 = jnp.bfloat16
F32 = jnp.float32

NZ = 8
NY = 8
CAP = 24
PAIR = 2 * CAP
ROWS = 4 * PAIR
TOK = 128
WIDTH = 1024
FF = 512
GU = 64
DN = 32
SEMS = 160

BEHIND = {1: 0, 2: 2, 3: 4, 4: 6, 5: 5, 6: 3, 7: 1}
AHEAD = {1: 1, 2: 3, 3: 5, 4: 6, 5: 4, 6: 2, 7: 0}
OPPOSITE, OWN = 6, 7


def flip(value, bit):
    size = 1 << bit
    return value + size - 2 * size * (lax.rem(lax.div(value, size), 2))


def dot(a, b, dims):
    return lax.dot_general(a, b, (dims, ((), ())), preferred_element_type=F32)


ROWS_COLS = ((1,), (0,))
LAST_LAST = ((1,), (1,))
FIRST_FIRST = ((0,), (0,))


def kernel(
    meta_ref, tok_ref, cot_ref, gu_ref, dn_ref, mate_ref,
    tg_out, gu_out, dn_out,
    gx, gc, gm, tri, sel, gcol, stx, stu, ex, eu, wgu, wdn, hb, qb, bk, rb,
    tgp, sz, rz, pgu, pdn, rygu, rydn, txgu, txdn, rxgu, rxdn, slgu, sldn, rlgu, rldn,
    ssem, rsem,
):
    dpi = lax.axis_index("dp")
    ei = lax.axis_index("expert")
    xl, y = lax.div(dpi, NY), lax.rem(dpi, NY)
    z, c = lax.div(ei, 4), lax.rem(ei, 4)

    def ydev(delta):
        return (xl * NY + lax.rem(y + delta + NY, NY), ei)

    def zdev(delta):
        return (dpi, lax.rem(z + delta + NZ, NZ) * 4 + c)

    column = [c, flip(c, 0), flip(c, 1), flip(flip(c, 0), 1)]
    plane = [(dpi, z * 4 + q) for q in column]
    other_side = ((1 - xl) * NY + y, ei)
    mates = [(dpi, flip(ei, bit)) for bit in range(5)]

    barrier = pltpu.get_barrier_semaphore()
    peers = [zdev(1), zdev(-1), mates[3], mates[4]] + plane[1:] + [ydev(1), ydev(-1), other_side]
    for peer in peers:
        pl.semaphore_signal(barrier, inc=1, device_id=peer, device_id_type=MESH)
    pl.semaphore_wait(barrier, len(peers))

    sent = []

    def send(src, dst, device, arrives=None):
        number = len(sent)
        copy = pltpu.make_async_remote_copy(
            src_ref=src,
            dst_ref=dst,
            send_sem=ssem.at[number],
            recv_sem=rsem.at[number],
            device_id=device,
            device_id_type=MESH,
        )
        copy.start()
        sent.append(copy)
        if arrives is None:
            return copy
        return pltpu.make_async_remote_copy(
            src_ref=arrives,
            dst_ref=arrives,
            send_sem=ssem.at[number],
            recv_sem=rsem.at[number],
            device_id=device,
            device_id_type=MESH,
        )

    def slice_at(ref, rows, side, delta):
        owner = side * NY + lax.rem(y + delta + NY, NY)
        return ref.at[pl.ds(pl.multiple_of(owner * rows, rows), rows)]

    sides = {"own": xl, "oth": 1 - xl}
    whole = {"gu": (wgu, GU, gu_ref), "dn": (wdn, DN, dn_ref)}
    reach = {("own", 1): 4, ("own", -1): 3, ("oth", 1): 3, ("oth", -1): 4}
    coming = {}

    def pass_weights(side, hop):
        for way in (1, -1):
            if hop > reach[side, way]:
                continue
            for kind, (buffer, rows, mine) in whole.items():
                if hop > 1:
                    coming[side, way, hop - 1, kind].wait_recv()
                source = slice_at(buffer, rows, sides[side], -way * (hop - 1))
                first = mine if hop == 1 and side == "own" else source
                coming[side, way, hop, kind] = send(
                    first, source, ydev(way), slice_at(buffer, rows, sides[side], -way * hop)
                )

    def last_weights(side):
        for way in (1, -1):
            for kind in whole:
                coming[side, way, reach[side, way], kind].wait_recv()

    across = {}
    for kind, (buffer, rows, mine) in whole.items():
        across[kind] = send(
            mine, slice_at(buffer, rows, xl, 0), other_side, slice_at(buffer, rows, 1 - xl, 0)
        )
    pass_weights("own", 1)

    def block(ref, index):
        return ref.at[pl.ds(index * TOK, TOK)]

    ring = {}

    def pass_meta(hop):
        if hop > 1:
            ring["m", 1, hop - 1].wait_recv()
            ring["m", -1, hop - 1].wait_recv()
        for way, order in ((1, BEHIND), (-1, AHEAD)):
            if hop > 3 and way < 0:
                continue
            source = meta_ref if hop == 1 else gm.at[order[hop - 1]]
            ring["m", way, hop] = send(source, gm.at[order[hop]], zdev(way))

    def pass_block(name, hop):
        mine, buffer = {"x": (tok_ref, gx), "c": (cot_ref, gc)}[name]
        if hop > 1:
            ring[name, 1, hop - 1].wait_recv()
            ring[name, -1, hop - 1].wait_recv()
        half = TOK // 2
        for way, order in ((1, BEHIND), (-1, AHEAD)):
            source = mine if hop == 1 else block(buffer, order[hop - 1])
            target = block(buffer, order[hop])
            if hop == 4:
                part = pl.ds(0 if way > 0 else half, half)
                source, target = source.at[part], target.at[part]
            ring[name, way, hop] = send(source, target, zdev(way))

    pass_meta(1)
    pass_block("x", 1)
    pass_block("c", 1)

    gx[OWN * TOK :, :] = tok_ref[...]
    gc[OWN * TOK :, :] = cot_ref[...]
    gm[OWN] = meta_ref[...]
    for kind, (buffer, rows, mine) in whole.items():
        slice_at(buffer, rows, xl, 0)[...] = mine[...]
    before = lax.broadcasted_iota(jnp.int32, (2 * TOK, 2 * TOK), 0)
    after = lax.broadcasted_iota(jnp.int32, (2 * TOK, 2 * TOK), 1)
    same_block = lax.div(before, TOK) == lax.div(after, TOK)
    tri[...] = jnp.where(same_block & (before < after), 1.0, 0.0).astype(BF16)

    def choose(pair):
        both = jnp.concatenate([gm[2 * pair], gm[2 * pair + 1]], axis=1)
        named, weight = both[0:4], both[4:8]
        hits, scales = [], []
        for q in column:
            hit = jnp.where(named == (z * 4 + q).astype(F32), 1.0, 0.0)
            hits.append(jnp.sum(hit, axis=0, keepdims=True))
            scales.append(jnp.sum(hit * weight, axis=0, keepdims=True))
        marks = jnp.concatenate(hits + [jnp.zeros((12, 2 * TOK), F32)], axis=0)
        ranks = dot(marks.astype(BF16), tri[...], ROWS_COLS)
        slot = lax.broadcasted_iota(jnp.int32, (CAP, 2 * TOK), 0).astype(F32)
        lane = lax.broadcasted_iota(jnp.int32, (CAP, 2 * TOK), 1)
        parts, columns = [], []
        for k in range(4):
            found = (ranks[k : k + 1] == slot) & (hits[k] > 0.5)
            for half in range(2):
                here = lane < TOK if half == 0 else lane >= TOK
                part = jnp.where(found & here, 1.0, 0.0)
                parts.append(part)
                columns.append(jnp.sum(part * scales[k], axis=1, keepdims=True))
        sel[pair] = jnp.concatenate(parts, axis=0).astype(BF16)
        gcol[pair] = jnp.broadcast_to(jnp.concatenate(columns, axis=0), (ROWS, 128))

    there = {}

    def dispatch(name, pair):
        buffer, staged, arrived = {"x": (gx, stx, ex), "c": (gc, stu, eu)}[name]
        for tile in range(0, WIDTH, 512):
            cols = pl.ds(tile, 512)
            rows = dot(sel[pair], buffer[2 * pair * TOK : 2 * (pair + 1) * TOK, cols], ROWS_COLS)
            if name == "c":
                rows = gcol[pair][:, 0:1] * rows
            rows = rows.astype(BF16)
            arrived[pair * ROWS : pair * ROWS + PAIR, cols] = rows[:PAIR]
            staged[pair * 3 * PAIR : (pair + 1) * 3 * PAIR, cols] = rows[PAIR:]
        for k in (2, 3, 1):
            there[name, pair, k] = send(
                staged.at[pl.ds((pair * 3 + k - 1) * PAIR, PAIR)],
                arrived.at[pl.ds((pair * 4 + k) * PAIR, PAIR)],
                plane[k],
            )

    returned = {}

    def expert(pair):
        for name in ("x", "c"):
            for k in (1, 2, 3):
                there[name, pair, k].wait_recv()
        rows = slice(pair * ROWS, (pair + 1) * ROWS)
        for tile in range(0, FF, 256):
            cols = pl.ds(tile, 256)
            up_cols = pl.ds(FF + tile, 256)
            a = dot(ex[rows], wgu[:, cols], ROWS_COLS)
            b = dot(ex[rows], wgu[:, up_cols], ROWS_COLS)
            dh = dot(eu[rows], wdn[cols], LAST_LAST)
            s = jax.nn.sigmoid(a)
            active = a * s
            hb[rows, cols] = (active * b).astype(BF16)
            qb[rows, cols] = (dh * b * (s * (1.0 + a * (1.0 - s)))).astype(BF16)
            qb[rows, up_cols] = (dh * active).astype(BF16)
        for tile in range(0, WIDTH, 256):
            cols = pl.ds(tile, 256)
            value = dot(qb[rows], wgu[cols], LAST_LAST).astype(BF16)
            bk[rows, cols] = value
            rb[pair * ROWS : pair * ROWS + PAIR, cols] = value[:PAIR]
        for k in (2, 3, 1):
            part = pl.ds((pair * 4 + k) * PAIR, PAIR)
            returned[pair, k] = send(bk.at[part], rb.at[part], plane[k])

    def combine(pair):
        for k in (1, 2, 3):
            returned[pair, k].wait_recv()
        for tile in range(0, WIDTH, 512):
            cols = pl.ds(tile, 512)
            tgp[pair * 256 : (pair + 1) * 256, cols] = dot(
                sel[pair], rb[pair * ROWS : (pair + 1) * ROWS, cols], FIRST_FIRST
            )

    ways = ((0, 1, BEHIND), (1, -1, AHEAD))
    sums = {}

    def token_step(step):
        for index, way, order in ways:
            if step > 1:
                sums[index, step - 1].wait_recv()
            first = order[step] * TOK
            term = tgp[first : first + TOK, index * 512 : (index + 1) * 512]
            if step == 1:
                sz[index] = term.astype(BF16)
                source = sz.at[index]
            else:
                source = rz.at[index, step - 2]
                source[...] = (source[...].astype(F32) + term).astype(BF16)
            sums[index, step] = send(source, rz.at[index, step - 1], zdev(way))

    def token_last():
        for index, _, _ in ways:
            sums[index, 7].wait_recv()
            cols = slice(index * 512, (index + 1) * 512)
            total = tgp[OWN * TOK :, cols] + rz[index, 6].astype(F32)
            tg_out[:, cols] = total.astype(BF16)

    partial = {"gu": (pgu, GU, rygu), "dn": (pdn, DN, rydn)}
    lanes = {("own", 1): 0, ("own", -1): 4, ("oth", 1): 7, ("oth", -1): 10}
    chain = {}

    def grad_step(kind, side, left):
        buffer, rows, received = partial[kind]
        for way in (1, -1):
            if left > reach[side, way]:
                continue
            term = slice_at(buffer, rows, sides[side], way * left)
            if left == reach[side, way]:
                source = term
            else:
                chain[kind, side, way, left + 1].wait_recv()
                source = received.at[lanes[side, way] + left]
                source[...] = (source[...].astype(F32) + term[...].astype(F32)).astype(BF16)
            chain[kind, side, way, left] = send(
                source, received.at[lanes[side, way] + left - 1], ydev(way)
            )

    def grad_sum(kind, side):
        buffer, rows, received = partial[kind]
        total = slice_at(buffer, rows, sides[side], 0)[...].astype(F32)
        for way in (1, -1):
            chain[kind, side, way, 1].wait_recv()
            total = total + received[lanes[side, way]].astype(F32)
        return total

    crossing = {"gu": (txgu, rxgu), "dn": (txdn, rxdn)}
    swaps = {"gu": (slgu, rlgu, gu_out), "dn": (sldn, rldn, dn_out)}
    crossed, moved = {}, {}

    def grad_cross(kind):
        outgoing, incoming = crossing[kind]
        outgoing[...] = grad_sum(kind, "oth").astype(BF16)
        crossed[kind] = send(outgoing, incoming, other_side)

    def grad_swap(kind):
        staged, landed, out = swaps[kind]
        total = grad_sum(kind, "own")
        crossed[kind].wait_recv()
        total = total + crossing[kind][1][...].astype(F32)
        out[...] = total
        staged[...] = total.astype(BF16)
        for bit in (4, 3, 2, 1, 0):
            moved[kind, bit] = send(staged, landed.at[bit], mates[bit])

    def grad_last(kind):
        _, landed, out = swaps[kind]
        mate = mate_ref[0]
        value = out[...]
        for bit in range(5):
            moved[kind, bit].wait_recv()
            value = jnp.where(mate == flip(ei, bit), landed[bit].astype(F32), value)
        out[...] = value

    def arrive_side():
        for kind in whole:
            across[kind].wait_recv()

    arrive_side()
    pass_weights("oth", 1)
    pass_weights("own", 2)
    pass_meta(2)
    pass_block("x", 2)
    choose(0)
    dispatch("x", 0)
    pass_weights("oth", 2)
    pass_block("c", 2)
    dispatch("c", 0)
    pass_weights("own", 3)
    pass_meta(3)
    pass_block("x", 3)
    choose(1)
    dispatch("x", 1)
    pass_weights("oth", 3)
    pass_block("c", 3)
    dispatch("c", 1)
    pass_weights("own", 4)
    pass_weights("oth", 4)
    pass_meta(4)
    pass_block("x", 4)
    choose(2)
    dispatch("x", 2)
    last_weights("own")
    last_weights("oth")
    ring["m", 1, 4].wait_recv()
    choose(3)
    pass_block("c", 4)
    dispatch("c", 2)
    expert(0)
    for way in (1, -1):
        ring["x", way, 4].wait_recv()
    dispatch("x", 3)
    for way in (1, -1):
        ring["c", way, 4].wait_recv()
    dispatch("c", 3)
    expert(1)
    expert(2)
    combine(0)
    token_step(1)
    combine(1)
    token_step(2)
    expert(3)
    for tile in range(0, FF, 256):
        cols = pl.ds(tile, 256)
        pdn[cols, :] = dot(hb[:, cols], eu[...], FIRST_FIRST).astype(BF16)
    grad_step("dn", "oth", 4)
    grad_step("dn", "own", 4)
    grad_step("dn", "oth", 3)
    grad_step("dn", "own", 3)
    for tile in range(0, WIDTH, 256):
        cols = pl.ds(tile, 256)
        pgu[cols, :] = dot(ex[:, cols], qb[...], FIRST_FIRST).astype(BF16)
    grad_step("gu", "oth", 4)
    grad_step("gu", "own", 4)
    grad_step("gu", "oth", 3)
    grad_step("gu", "own", 3)
    combine(2)
    token_step(3)
    combine(3)
    token_step(4)
    grad_step("dn", "oth", 2)
    grad_step("dn", "own", 2)
    token_step(5)
    grad_step("gu", "oth", 2)
    grad_step("gu", "own", 2)
    token_step(6)
    grad_step("dn", "oth", 1)
    grad_step("dn", "own", 1)
    token_step(7)
    grad_step("gu", "oth", 1)
    grad_step("gu", "own", 1)
    token_last()
    grad_cross("dn")
    grad_swap("dn")
    grad_cross("gu")
    grad_swap("gu")
    grad_last("dn")
    grad_last("gu")
    for copy in sent:
        copy.wait_send()
    assert len(sent) <= SEMS


def table_lookup(keys, table):
    hits = keys[..., None] == jnp.arange(table.shape[0], dtype=jnp.int32)
    return jnp.sum(jnp.where(hits, table, 0), axis=-1)


def body(tokens, cotangent, gates, expert_ids, placement, partner, w_gate_up, w_down):
    here = lax.axis_index("expert")
    mate = lax.dynamic_slice_in_dim(partner, here, 1)
    holder = table_lookup(expert_ids, table_lookup(placement, partner))
    meta = jnp.concatenate([holder.astype(F32).T, gates.T], axis=0)

    def vmem(*shape, dtype=BF16):
        return pltpu.VMEM(shape, dtype)

    slots = 4 * ROWS
    scratch = [
        vmem(NZ * TOK, WIDTH),
        vmem(NZ * TOK, WIDTH),
        vmem(NZ, 8, TOK, dtype=F32),
        vmem(2 * TOK, 2 * TOK),
        vmem(4, ROWS, 2 * TOK),
        vmem(4, ROWS, 128, dtype=F32),
        vmem(12 * PAIR, WIDTH),
        vmem(12 * PAIR, WIDTH),
        vmem(slots, WIDTH),
        vmem(slots, WIDTH),
        vmem(WIDTH, 2 * FF),
        vmem(FF, WIDTH),
        vmem(slots, FF),
        vmem(slots, 2 * FF),
        vmem(slots, WIDTH),
        vmem(slots, WIDTH),
        vmem(NZ * TOK, WIDTH, dtype=F32),
        vmem(2, TOK, 512),
        vmem(2, 7, TOK, 512),
        vmem(WIDTH, 2 * FF),
        vmem(FF, WIDTH),
        vmem(14, GU, 2 * FF),
        vmem(14, DN, WIDTH),
        vmem(GU, 2 * FF),
        vmem(DN, WIDTH),
        vmem(GU, 2 * FF),
        vmem(DN, WIDTH),
        vmem(GU, 2 * FF),
        vmem(DN, WIDTH),
        vmem(5, GU, 2 * FF),
        vmem(5, DN, WIDTH),
        pltpu.SemaphoreType.DMA((SEMS,)),
        pltpu.SemaphoreType.DMA((SEMS,)),
    ]
    in_vmem = pl.BlockSpec(memory_space=pltpu.VMEM)
    token_grad, grad_gu, grad_dn = pl.pallas_call(
        kernel,
        out_shape=(
            jax.ShapeDtypeStruct((TOK, WIDTH), BF16),
            jax.ShapeDtypeStruct((GU, 2 * FF), F32),
            jax.ShapeDtypeStruct((DN, WIDTH), F32),
        ),
        in_specs=[in_vmem] * 5 + [pl.BlockSpec(memory_space=pltpu.SMEM)],
        out_specs=(in_vmem,) * 3,
        scratch_shapes=scratch,
        compiler_params=pltpu.CompilerParams(
            collective_id=0, has_side_effects=True, vmem_limit_bytes=56 * 1024 * 1024
        ),
    )(meta, tokens, cotangent, w_gate_up[0], w_down[0], mate)
    return token_grad, grad_gu[None], grad_dn[None]


def solution(mesh):
    return jax.shard_map(
        body,
        mesh=mesh,
        in_specs=(
            P(("dp", "expert"), None),
            P(("dp", "expert"), None),
            P(("dp", "expert"), None),
            P(("dp", "expert"), None),
            P(),
            P(),
            P("expert", "dp", None),
            P("expert", "dp", None),
        ),
        out_specs=(P(("dp", "expert"), None), P("expert", "dp", None), P("expert", "dp", None)),
        check_vma=False,
    )
```

```python
import functools

import jax
import jax.numpy as jnp
from jax import lax
from jax.experimental import pallas as pl
from jax.experimental.pallas import tpu as pltpu
from jax.sharding import PartitionSpec as P

MESH = pl.DeviceIdType.MESH
BF16 = jnp.bfloat16
F32 = jnp.float32

NZ = 8
NY = 8
CAP = 24
PAIR = 2 * CAP
ROWS = 4 * PAIR
TOK = 128
WIDTH = 1024
FF = 512
GU = 64
DN = 32
PART = 32
SEMS = 192

BEHIND = {1: 0, 2: 2, 3: 4, 4: 6, 5: 5, 6: 3, 7: 1}
AHEAD = {1: 1, 2: 3, 3: 5, 4: 6, 5: 4, 6: 2, 7: 0}
OPPOSITE, OWN = 6, 7


def flip(value, bit):
    size = 1 << bit
    return value + size - 2 * size * (lax.rem(lax.div(value, size), 2))


def dot(a, b, dims):
    return lax.dot_general(a, b, (dims, ((), ())), preferred_element_type=F32)


ROWS_COLS = ((1,), (0,))
LAST_LAST = ((1,), (1,))
FIRST_FIRST = ((0,), (0,))


def kernel(
    ids_ref, gates_ref, tok_ref, cot_ref, gu_ref, dn_ref, placement_ref, partner_ref,
    tg_out, gu_out, dn_out,
    gx, gc, gm, tri, sel, gcol, stx, stu, ex, eu, wgu, wdn, hb, qb, bk, rb,
    tgp, sz, rz, agu, adn, pgu, pdn, ry, tx, rx, sl, rl, tgb, gub, dnb,
    ssem, rsem, lsem,
):
    dpi = lax.axis_index("dp")
    ei = lax.axis_index("expert")
    xl, y = lax.div(dpi, NY), lax.rem(dpi, NY)
    z, c = lax.div(ei, 4), lax.rem(ei, 4)

    def ydev(delta):
        return (xl * NY + lax.rem(y + delta + NY, NY), ei)

    def zdev(delta):
        return (dpi, lax.rem(z + delta + NZ, NZ) * 4 + c)

    column = [c, flip(c, 0), flip(c, 1), flip(flip(c, 0), 1)]
    plane = [(dpi, z * 4 + q) for q in column]
    other_side = ((1 - xl) * NY + y, ei)
    mates = [(dpi, flip(ei, bit)) for bit in range(5)]

    barrier = pltpu.get_barrier_semaphore()
    peers = [zdev(1), zdev(-1), mates[3], mates[4]] + plane[1:] + [ydev(1), ydev(-1), other_side]
    for peer in peers:
        pl.semaphore_signal(barrier, inc=1, device_id=peer, device_id_type=MESH)
    pl.semaphore_wait(barrier, len(peers))

    sent = []

    local = []

    def move(src, dst):
        copy = pltpu.make_async_copy(src, dst, lsem.at[len(local)])
        copy.start()
        local.append(copy)
        return copy

    def send(src, dst, device, arrives=None):
        number = len(sent)
        copy = pltpu.make_async_remote_copy(
            src_ref=src,
            dst_ref=dst,
            send_sem=ssem.at[number],
            recv_sem=rsem.at[number],
            device_id=device,
            device_id_type=MESH,
        )
        copy.start()
        sent.append(copy)
        if arrives is None:
            return copy
        return pltpu.make_async_remote_copy(
            src_ref=arrives,
            dst_ref=arrives,
            send_sem=ssem.at[number],
            recv_sem=rsem.at[number],
            device_id=device,
            device_id_type=MESH,
        )

    def slice_at(ref, rows, side, delta):
        owner = side * NY + lax.rem(y + delta + NY, NY)
        return ref.at[pl.ds(pl.multiple_of(owner * rows, rows), rows)]

    sides = {"own": xl, "oth": 1 - xl}
    whole = {"gu": (wgu, GU, gu_ref.at[0]), "dn": (wdn, DN, dn_ref.at[0])}
    reach = {("own", 1): 4, ("own", -1): 3, ("oth", 1): 3, ("oth", -1): 4}
    coming = {}

    def pass_weights(side, hop):
        for way in (1, -1):
            if hop > reach[side, way]:
                continue
            for kind, (buffer, rows, mine) in whole.items():
                if hop > 1:
                    coming[side, way, hop - 1, kind].wait_recv()
                source = slice_at(buffer, rows, sides[side], -way * (hop - 1))
                first = mine if hop == 1 and side == "own" else source
                coming[side, way, hop, kind] = send(
                    first, source, ydev(way), slice_at(buffer, rows, sides[side], -way * hop)
                )

    def last_weights(side):
        for way in (1, -1):
            for kind in whole:
                coming[side, way, reach[side, way], kind].wait_recv()

    across = {}
    for kind, (buffer, rows, mine) in whole.items():
        across[kind] = send(
            mine, slice_at(buffer, rows, xl, 0), other_side, slice_at(buffer, rows, 1 - xl, 0)
        )
    pass_weights("own", 1)

    def block(ref, index):
        return ref.at[pl.ds(index * TOK, TOK)]

    ring = {}

    def pass_meta(hop):
        if hop > 1:
            ring["m", 1, hop - 1].wait_recv()
            ring["m", -1, hop - 1].wait_recv()
        for way, order in ((1, BEHIND), (-1, AHEAD)):
            if hop > 3 and way < 0:
                continue
            source = gm.at[OWN if hop == 1 else order[hop - 1]]
            ring["m", way, hop] = send(source, gm.at[order[hop]], zdev(way))

    def pass_block(name, hop):
        mine, buffer = {"x": (tok_ref, gx), "c": (cot_ref, gc)}[name]
        if hop > 1:
            ring[name, 1, hop - 1].wait_recv()
            ring[name, -1, hop - 1].wait_recv()
        half = TOK // 2
        for way, order in ((1, BEHIND), (-1, AHEAD)):
            source = mine if hop == 1 else block(buffer, order[hop - 1])
            target = block(buffer, order[hop])
            if hop == 4:
                part = pl.ds(0 if way > 0 else half, half)
                source, target = source.at[part], target.at[part]
            ring[name, way, hop] = send(source, target, zdev(way))

    ids = ids_ref[...]
    holder = jnp.zeros(ids.shape, F32)
    for e in range(32):
        holder = jnp.where(ids == e, partner_ref[placement_ref[e]].astype(F32), holder)
    gm[OWN, 0:4, :] = holder
    gm[OWN, 4:8, :] = gates_ref[...]
    pass_meta(1)
    pass_block("x", 1)
    pass_block("c", 1)
    own_parts = [move(tok_ref, block(gx, OWN)), move(cot_ref, block(gc, OWN))]
    for kind, (buffer, rows, mine) in whole.items():
        own_parts.append(move(mine, slice_at(buffer, rows, xl, 0)))

    before = lax.broadcasted_iota(jnp.int32, (2 * TOK, 2 * TOK), 0)
    after = lax.broadcasted_iota(jnp.int32, (2 * TOK, 2 * TOK), 1)
    same_block = lax.div(before, TOK) == lax.div(after, TOK)
    tri[...] = jnp.where(same_block & (before < after), 1.0, 0.0).astype(BF16)

    def choose(pair):
        both = jnp.concatenate([gm[2 * pair], gm[2 * pair + 1]], axis=1)
        named, weight = both[0:4], both[4:8]
        hits, scales = [], []
        for q in column:
            hit = jnp.where(named == (z * 4 + q).astype(F32), 1.0, 0.0)
            hits.append(jnp.sum(hit, axis=0, keepdims=True))
            scales.append(jnp.sum(hit * weight, axis=0, keepdims=True))
        marks = jnp.concatenate(hits + [jnp.zeros((12, 2 * TOK), F32)], axis=0)
        ranks = dot(marks.astype(BF16), tri[...], ROWS_COLS)
        slot = lax.broadcasted_iota(jnp.int32, (CAP, 2 * TOK), 0).astype(F32)
        lane = lax.broadcasted_iota(jnp.int32, (CAP, 2 * TOK), 1)
        parts, columns = [], []
        for k in range(4):
            found = (ranks[k : k + 1] == slot) & (hits[k] > 0.5)
            for half in range(2):
                here = lane < TOK if half == 0 else lane >= TOK
                part = jnp.where(found & here, 1.0, 0.0)
                parts.append(part)
                columns.append(jnp.sum(part * scales[k], axis=1, keepdims=True))
        sel[pair] = jnp.concatenate(parts, axis=0).astype(BF16)
        gcol[pair] = jnp.broadcast_to(jnp.concatenate(columns, axis=0), (ROWS, 128))

    there = {}

    def dispatch(name, pair):
        buffer, staged, arrived = {"x": (gx, stx, ex), "c": (gc, stu, eu)}[name]
        for tile in range(0, WIDTH, 512):
            cols = pl.ds(tile, 512)
            rows = dot(sel[pair], buffer[2 * pair * TOK : 2 * (pair + 1) * TOK, cols], ROWS_COLS)
            if name == "c":
                rows = gcol[pair][:, 0:1] * rows
            rows = rows.astype(BF16)
            arrived[pair * ROWS : pair * ROWS + PAIR, cols] = rows[:PAIR]
            staged[pair * 3 * PAIR : (pair + 1) * 3 * PAIR, cols] = rows[PAIR:]
        for k in (2, 3, 1):
            there[name, pair, k] = send(
                staged.at[pl.ds((pair * 3 + k - 1) * PAIR, PAIR)],
                arrived.at[pl.ds((pair * 4 + k) * PAIR, PAIR)],
                plane[k],
            )

    returned = {}

    def rows_here(pair):
        for name in ("x", "c"):
            for k in (1, 2, 3):
                there[name, pair, k].wait_recv()

    def expert(pair):
        rows = slice(pair * ROWS, (pair + 1) * ROWS)
        for tile in range(0, FF, 256):
            cols = pl.ds(tile, 256)
            up_cols = pl.ds(FF + tile, 256)
            a = dot(ex[rows], wgu[:, cols], ROWS_COLS)
            b = dot(ex[rows], wgu[:, up_cols], ROWS_COLS)
            dh = dot(eu[rows], wdn[cols], LAST_LAST)
            s = jax.nn.sigmoid(a)
            active = a * s
            hb[rows, cols] = (active * b).astype(BF16)
            qb[rows, cols] = (dh * b * (s * (1.0 + a * (1.0 - s)))).astype(BF16)
            qb[rows, up_cols] = (dh * active).astype(BF16)
        for tile in range(0, WIDTH, 256):
            cols = pl.ds(tile, 256)
            value = dot(qb[rows], wgu[cols], LAST_LAST).astype(BF16)
            bk[rows, cols] = value
            rb[pair * ROWS : pair * ROWS + PAIR, cols] = value[:PAIR]

    def give_back(pair):
        for k in (2, 3, 1):
            part = pl.ds((pair * 4 + k) * PAIR, PAIR)
            returned[pair, k] = send(bk.at[part], rb.at[part], plane[k])

    def combine(pair):
        for k in (1, 2, 3):
            returned[pair, k].wait_recv()
        for tile in range(0, WIDTH, 512):
            cols = pl.ds(tile, 512)
            tgp[pair * 256 : (pair + 1) * 256, cols] = dot(
                sel[pair], rb[pair * ROWS : (pair + 1) * ROWS, cols], FIRST_FIRST
            )

    ways = ((0, 1, BEHIND), (1, -1, AHEAD))
    sums = {}

    def token_step(step):
        for index, way, order in ways:
            if step > 1:
                sums[index, step - 1].wait_recv()
            first = order[step] * TOK
            term = tgp[first : first + TOK, index * 512 : (index + 1) * 512]
            if step == 1:
                sz[index] = term.astype(BF16)
                source = sz.at[index]
            else:
                source = rz.at[index, step - 2]
                source[...] = (source[...].astype(F32) + term).astype(BF16)
            sums[index, step] = send(source, rz.at[index, step - 1], zdev(way))

    def token_last():
        for index, _, _ in ways:
            sums[index, 7].wait_recv()
            cols = slice(index * 512, (index + 1) * 512)
            total = tgp[OWN * TOK :, cols] + rz[index, 6].astype(F32)
            tgb[:, cols] = total.astype(BF16)
        move(tgb, tg_out)

    parts = {"dn": (pdn, DN, 0, 0), "g0": (pgu, GU, 0, 1), "g1": (pgu, GU, PART, 2)}
    lanes = {("own", 1): 0, ("own", -1): 4, ("oth", 1): 7, ("oth", -1): 10}
    chain = {}

    def part_at(kind, side, delta):
        buffer, rows, first, _ = parts[kind]
        owner = sides[side] * NY + lax.rem(y + delta + NY, NY)
        return buffer.at[pl.ds(pl.multiple_of(owner * rows + first, PART), PART)]

    def grad_step(kind, side, way, left):
        received = ry.at[parts[kind][3]]
        term = part_at(kind, side, way * left)
        if left == reach[side, way]:
            source = term
        else:
            chain[kind, side, way, left + 1].wait_recv()
            source = received.at[lanes[side, way] + left]
            source[...] = (source[...].astype(F32) + term[...].astype(F32)).astype(BF16)
        chain[kind, side, way, left] = send(
            source, received.at[lanes[side, way] + left - 1], ydev(way)
        )

    def grad_round(kind, number):
        if number == 1:
            grad_step(kind, "oth", 1, 3)
            grad_step(kind, "oth", -1, 4)
            grad_step(kind, "own", 1, 4)
            grad_step(kind, "own", -1, 3)
        elif number == 2:
            grad_step(kind, "oth", 1, 2)
            grad_step(kind, "oth", -1, 3)
            grad_step(kind, "own", 1, 3)
            grad_step(kind, "own", -1, 2)
        elif number == 3:
            grad_step(kind, "oth", 1, 1)
            grad_step(kind, "oth", -1, 2)
            grad_step(kind, "own", 1, 2)
            grad_step(kind, "own", -1, 1)
        else:
            grad_step(kind, "oth", -1, 1)
            grad_step(kind, "own", 1, 1)

    def grad_sum(kind, side):
        total = part_at(kind, side, 0)[...].astype(F32)
        for way in (1, -1):
            chain[kind, side, way, 1].wait_recv()
            total = total + ry[parts[kind][3], lanes[side, way]].astype(F32)
        return total

    results = {"dn": (dnb, dn_out, 0), "g0": (gub, gu_out, 0), "g1": (gub, gu_out, PART)}
    crossed, moved = {}, {}

    def grad_cross(kind):
        index = parts[kind][3]
        tx[index] = grad_sum(kind, "oth").astype(BF16)
        crossed[kind] = send(tx.at[index], rx.at[index], other_side)

    def grad_swap(kind):
        index = parts[kind][3]
        kept, _, first = results[kind]
        total = grad_sum(kind, "own")
        crossed[kind].wait_recv()
        total = total + rx[index].astype(F32)
        kept[first : first + PART, :] = total
        sl[index] = total.astype(BF16)
        for bit in (4, 3, 2, 1, 0):
            moved[kind, bit] = send(sl.at[index], rl.at[index, bit], mates[bit])

    def grad_last(kind):
        kept, out, first = results[kind]
        mate = partner_ref[ei]
        value = kept[first : first + PART, :]
        for bit in range(5):
            moved[kind, bit].wait_recv()
            landed = rl[parts[kind][3], bit].astype(F32)
            value = jnp.where(mate == flip(ei, bit), landed, value)
        kept[first : first + PART, :] = value
        rows = pl.ds(first, PART)
        move(kept.at[rows], out.at[rows])

    early = 3 * ROWS

    def ahead_of_last():
        for tile in range(0, FF, 256):
            cols = pl.ds(tile, 256)
            adn[cols, :] = dot(hb[0:early, cols], eu[0:early], FIRST_FIRST)
        for tile in range(0, WIDTH, 256):
            cols = pl.ds(tile, 256)
            agu[cols, :] = dot(ex[0:early, cols], qb[0:early], FIRST_FIRST)

    def last_dn():
        for tile in range(0, FF, 256):
            cols = pl.ds(tile, 256)
            term = dot(hb[early:, cols], eu[early:], FIRST_FIRST)
            pdn[cols, :] = (adn[cols, :] + term).astype(BF16)

    def last_gu():
        for tile in range(0, WIDTH, 256):
            cols = pl.ds(tile, 256)
            term = dot(ex[early:, cols], qb[early:], FIRST_FIRST)
            pgu[cols, :] = (agu[cols, :] + term).astype(BF16)

    def arrive_side():
        for kind in whole:
            across[kind].wait_recv()

    arrive_side()
    pass_weights("oth", 1)
    pass_weights("own", 2)
    pass_meta(2)
    pass_block("x", 2)
    choose(0)
    dispatch("x", 0)
    pass_weights("oth", 2)
    pass_block("c", 2)
    dispatch("c", 0)
    pass_weights("own", 3)
    pass_meta(3)
    pass_block("x", 3)
    choose(1)
    dispatch("x", 1)
    pass_weights("oth", 3)
    pass_block("c", 3)
    dispatch("c", 1)
    pass_weights("own", 4)
    pass_weights("oth", 4)
    pass_meta(4)
    pass_block("x", 4)
    choose(2)
    dispatch("x", 2)
    ring["m", 1, 4].wait_recv()
    choose(3)
    for copy in own_parts:
        copy.wait()
    pass_block("c", 4)
    dispatch("c", 2)
    last_weights("own")
    last_weights("oth")
    rows_here(0)
    expert(0)
    for way in (1, -1):
        ring["x", way, 4].wait_recv()
    dispatch("x", 3)
    rows_here(1)
    expert(1)
    for way in (1, -1):
        ring["c", way, 4].wait_recv()
    dispatch("c", 3)
    rows_here(2)
    expert(2)
    ahead_of_last()
    rows_here(3)
    give_back(0)
    give_back(1)
    expert(3)
    last_dn()
    grad_round("dn", 1)
    last_gu()
    grad_round("g0", 1)
    give_back(2)
    give_back(3)
    combine(0)
    token_step(1)
    grad_round("dn", 2)
    grad_round("g0", 2)
    combine(1)
    token_step(2)
    grad_round("dn", 3)
    grad_round("g1", 1)
    combine(2)
    token_step(3)
    grad_round("dn", 4)
    grad_round("g0", 3)
    combine(3)
    token_step(4)
    grad_cross("dn")
    grad_round("g1", 2)
    token_step(5)
    grad_round("g0", 4)
    grad_swap("dn")
    token_step(6)
    grad_round("g1", 3)
    grad_cross("g0")
    token_step(7)
    grad_round("g1", 4)
    grad_swap("g0")
    grad_cross("g1")
    token_last()
    grad_swap("g1")
    grad_last("dn")
    grad_last("g0")
    grad_last("g1")
    for copy in local[len(own_parts) :]:
        copy.wait()
    for copy in sent:
        copy.wait_send()
    assert len(sent) <= SEMS


def hand_on(*refs):
    count = len(refs) // 3
    sources, results, held = refs[:count], refs[count : 2 * count], refs[2 * count : 3 * count]
    arriving, leaving = refs[3 * count :]
    copies = []
    for index in range(count):
        copies.append(pltpu.make_async_copy(sources[index], held[index], arriving.at[index]))
        copies[index].start()
    for index in range(count):
        copies[index].wait()
        target = results[index] if index == 0 else results[index].at[0]
        copies[index] = pltpu.make_async_copy(held[index], target, leaving.at[index])
        copies[index].start()
    for copy in copies:
        copy.wait()


def body(tokens, cotangent, gates, expert_ids, placement, partner, w_gate_up, w_down):
    def vmem(*shape, dtype=BF16):
        return pltpu.VMEM(shape, dtype)

    slots = 4 * ROWS
    scratch = [
        vmem(NZ * TOK, WIDTH),
        vmem(NZ * TOK, WIDTH),
        vmem(NZ, 8, TOK, dtype=F32),
        vmem(2 * TOK, 2 * TOK),
        vmem(4, ROWS, 2 * TOK),
        vmem(4, ROWS, 128, dtype=F32),
        vmem(12 * PAIR, WIDTH),
        vmem(12 * PAIR, WIDTH),
        vmem(slots, WIDTH),
        vmem(slots, WIDTH),
        vmem(WIDTH, 2 * FF),
        vmem(FF, WIDTH),
        vmem(slots, FF),
        vmem(slots, 2 * FF),
        vmem(slots, WIDTH),
        vmem(slots, WIDTH),
        vmem(NZ * TOK, WIDTH, dtype=F32),
        vmem(2, TOK, 512),
        vmem(2, 7, TOK, 512),
        vmem(WIDTH, 2 * FF, dtype=F32),
        vmem(FF, WIDTH, dtype=F32),
        vmem(WIDTH, 2 * FF),
        vmem(FF, WIDTH),
        vmem(3, 14, PART, WIDTH),
        vmem(3, PART, WIDTH),
        vmem(3, PART, WIDTH),
        vmem(3, PART, WIDTH),
        vmem(3, 5, PART, WIDTH),
        vmem(TOK, WIDTH),
        vmem(GU, 2 * FF, dtype=F32),
        vmem(DN, WIDTH, dtype=F32),
        pltpu.SemaphoreType.DMA((SEMS,)),
        pltpu.SemaphoreType.DMA((SEMS,)),
        pltpu.SemaphoreType.DMA((8,)),
    ]
    in_vmem = pl.BlockSpec(memory_space=pltpu.VMEM)
    in_smem = pl.BlockSpec(memory_space=pltpu.SMEM)
    anywhere = pl.BlockSpec(memory_space=pl.ANY)
    results = pl.pallas_call(
        kernel,
        out_shape=(
            jax.ShapeDtypeStruct((TOK, WIDTH), BF16),
            jax.ShapeDtypeStruct((GU, 2 * FF), F32),
            jax.ShapeDtypeStruct((DN, WIDTH), F32),
        ),
        in_specs=[in_vmem] * 2 + [anywhere] * 4 + [in_smem] * 2,
        out_specs=(anywhere,) * 3,
        scratch_shapes=scratch,
        compiler_params=pltpu.CompilerParams(
            collective_id=0, has_side_effects=True, vmem_limit_bytes=58 * 1024 * 1024
        ),
    )(expert_ids.T, gates.T, tokens, cotangent, w_gate_up, w_down, placement, partner)
    return pl.pallas_call(
        hand_on,
        out_shape=(
            jax.ShapeDtypeStruct((TOK, WIDTH), BF16),
            jax.ShapeDtypeStruct((1, GU, 2 * FF), F32),
            jax.ShapeDtypeStruct((1, DN, WIDTH), F32),
        ),
        in_specs=[anywhere] * 3,
        out_specs=(anywhere,) * 3,
        scratch_shapes=[
            vmem(TOK, WIDTH),
            vmem(GU, 2 * FF, dtype=F32),
            vmem(DN, WIDTH, dtype=F32),
            pltpu.SemaphoreType.DMA((3,)),
            pltpu.SemaphoreType.DMA((3,)),
        ],
        compiler_params=pltpu.CompilerParams(vmem_limit_bytes=58 * 1024 * 1024),
    )(*results)


def solution(mesh):
    return jax.shard_map(
        body,
        mesh=mesh,
        in_specs=(
            P(("dp", "expert"), None),
            P(("dp", "expert"), None),
            P(("dp", "expert"), None),
            P(("dp", "expert"), None),
            P(),
            P(),
            P("expert", "dp", None),
            P("expert", "dp", None),
        ),
        out_specs=(P(("dp", "expert"), None), P("expert", "dp", None), P("expert", "dp", None)),
        check_vma=False,
    )
```

```python
import math

import jax
import jax.numpy as jnp
from jax import lax
from jax.experimental import pallas as pl
from jax.experimental.pallas import tpu as pltpu
from jax.sharding import PartitionSpec as P

MESH = pl.DeviceIdType.MESH
BF16 = jnp.bfloat16
F32 = jnp.float32

NZ = 8
NY = 8
CAP = 24
PAIR = 2 * CAP
ROWS = 4 * PAIR
TOK = 128
WIDTH = 1024
FF = 512
GU = 64
DN = 32
PARTS = (32, 32, 32)
RECEIVES = 89
GROUPS = ("weights", "meta", "ring", "out", "back", "sums", "grads", "swap", "pieces")

BEHIND = {1: 0, 2: 2, 3: 4, 4: 6, 5: 5, 6: 3, 7: 1}
AHEAD = {1: 1, 2: 3, 3: 5, 4: 6, 5: 4, 6: 2, 7: 0}
OPPOSITE, OWN = 6, 7


def flip(value, bit):
    size = 1 << bit
    return value + size - 2 * size * (lax.rem(lax.div(value, size), 2))


def dot(a, b, dims):
    return lax.dot_general(a, b, (dims, ((), ())), preferred_element_type=F32)


ROWS_COLS = ((1,), (0,))
LAST_LAST = ((1,), (1,))
FIRST_FIRST = ((0,), (0,))


def kernel(
    ids_ref, gates_ref, tok_ref, cot_ref, gu_ref, dn_ref, placement_ref, partner_ref,
    tg_out, gu_out, dn_out,
    gx, gc, gm, tri, sel, gcol, stx, stu, ex, eu, wgu, wdn, hb, qb, bk, rb,
    tgp, sz, rz, agu, adn, pgu, pdn, ry, tx, rx, sl, rl, cut, via, onward, whence, tgb, gub, dnb,
    ssem, rsem, lsem,
):
    dpi = lax.axis_index("dp")
    ei = lax.axis_index("expert")
    xl, y = lax.div(dpi, NY), lax.rem(dpi, NY)
    z, c = lax.div(ei, 4), lax.rem(ei, 4)

    def ydev(delta):
        return (xl * NY + lax.rem(y + delta + NY, NY), ei)

    def zdev(delta):
        return (dpi, lax.rem(z + delta + NZ, NZ) * 4 + c)

    column = [c, flip(c, 0), flip(c, 1), flip(flip(c, 0), 1)]
    plane = [(dpi, z * 4 + q) for q in column]
    other_side = ((1 - xl) * NY + y, ei)

    barrier = pltpu.get_barrier_semaphore()
    peers = [zdev(r) for r in range(1, NZ)] + plane[1:] + [ydev(1), ydev(-1), other_side]
    for peer in peers:
        pl.semaphore_signal(barrier, inc=1, device_id=peer, device_id_type=MESH)
    pl.semaphore_wait(barrier, len(peers))

    sent = {group: [] for group in GROUPS}
    receives = []

    local = []

    def move(src, dst):
        copy = pltpu.make_async_copy(src, dst, lsem.at[len(local)])
        copy.start()
        local.append(copy)
        return copy

    def new():
        receives.append(len(receives))
        return receives[-1]

    def send(group, receive, src, dst, device):
        copy = pltpu.make_async_remote_copy(
            src_ref=src,
            dst_ref=dst,
            send_sem=ssem.at[GROUPS.index(group)],
            recv_sem=rsem.at[receive],
            device_id=device,
            device_id_type=MESH,
        )
        copy.start()
        sent[group].append(src)

    def arrive(receive, ref):
        pltpu.make_async_remote_copy(
            src_ref=ref,
            dst_ref=ref,
            send_sem=ssem.at[0],
            recv_sem=rsem.at[receive],
            device_id=other_side,
            device_id_type=MESH,
        ).wait_recv()

    def slice_at(ref, rows, side, delta):
        owner = side * NY + lax.rem(y + delta + NY, NY)
        return ref.at[pl.ds(pl.multiple_of(owner * rows, rows), rows)]

    sides = {"own": xl, "oth": 1 - xl}
    whole = {"gu": (wgu, GU, gu_ref.at[0]), "dn": (wdn, DN, dn_ref.at[0])}
    reach = {("own", 1): 4, ("own", -1): 3, ("oth", 1): 3, ("oth", -1): 4}
    coming = {}
    one_slice = wgu.at[pl.ds(0, GU + DN)]

    def pass_weights(side, hop):
        for way in (1, -1):
            if hop > reach[side, way]:
                continue
            if hop > 1:
                arrive(coming[side, way, hop - 1], one_slice)
            coming[side, way, hop] = new()
            for buffer, rows, mine in whole.values():
                target = slice_at(buffer, rows, sides[side], -way * (hop - 1))
                source = mine if hop == 1 and side == "own" else target
                send("weights", coming[side, way, hop], source, target, ydev(way))

    def last_weights(side):
        for way in (1, -1):
            arrive(coming[side, way, reach[side, way]], one_slice)

    across = new()
    for buffer, rows, mine in whole.values():
        send("weights", across, mine, slice_at(buffer, rows, xl, 0), other_side)
    pass_weights("own", 1)

    def block(ref, index):
        return ref.at[pl.ds(index * TOK, TOK)]

    ring = {}

    def pass_meta(hop):
        if hop > 1:
            arrive(ring["m", hop - 1], gm.at[pl.ds(2 * hop - 4, 2)])
        ring["m", hop] = new()
        for way, order in ((1, BEHIND), (-1, AHEAD)):
            if hop > 3 and way < 0:
                continue
            source = gm.at[OWN if hop == 1 else order[hop - 1]]
            send("meta", ring["m", hop], source, gm.at[order[hop]], zdev(way))

    def block_here(name, hop):
        buffer = gx if name == "x" else gc
        arrive(ring[name, hop], buffer.at[pl.ds(2 * (hop - 1) * TOK, TOK if hop == 4 else 2 * TOK)])

    def pass_block(name, hop):
        mine, buffer = {"x": (tok_ref, gx), "c": (cot_ref, gc)}[name]
        if hop > 1:
            block_here(name, hop - 1)
        half = TOK // 2
        ring[name, hop] = new()
        for way, order in ((1, BEHIND), (-1, AHEAD)):
            source = mine if hop == 1 else block(buffer, order[hop - 1])
            target = block(buffer, order[hop])
            if hop == 4:
                part = pl.ds(0 if way > 0 else half, half)
                source, target = source.at[part], target.at[part]
            send("ring", ring[name, hop], source, target, zdev(way))

    ids = ids_ref[...]
    holder = jnp.zeros(ids.shape, F32)
    for e in range(32):
        holder = jnp.where(ids == e, partner_ref[placement_ref[e]].astype(F32), holder)
    gm[OWN, 0:4, :] = holder
    gm[OWN, 4:8, :] = gates_ref[...]
    pass_meta(1)
    pass_block("x", 1)
    pass_block("c", 1)
    own_parts = [move(tok_ref, block(gx, OWN)), move(cot_ref, block(gc, OWN))]
    for buffer, rows, mine in whole.values():
        own_parts.append(move(mine, slice_at(buffer, rows, xl, 0)))

    before = lax.broadcasted_iota(jnp.int32, (2 * TOK, 2 * TOK), 0)
    after = lax.broadcasted_iota(jnp.int32, (2 * TOK, 2 * TOK), 1)
    same_block = lax.div(before, TOK) == lax.div(after, TOK)
    tri[...] = jnp.where(same_block & (before < after), 1.0, 0.0).astype(BF16)

    def choose(pair):
        both = jnp.concatenate([gm[2 * pair], gm[2 * pair + 1]], axis=1)
        named, weight = both[0:4], both[4:8]
        hits, scales = [], []
        for q in column:
            hit = jnp.where(named == (z * 4 + q).astype(F32), 1.0, 0.0)
            hits.append(jnp.sum(hit, axis=0, keepdims=True))
            scales.append(jnp.sum(hit * weight, axis=0, keepdims=True))
        marks = jnp.concatenate(hits + [jnp.zeros((12, 2 * TOK), F32)], axis=0)
        ranks = dot(marks.astype(BF16), tri[...], ROWS_COLS)
        slot = lax.broadcasted_iota(jnp.int32, (CAP, 2 * TOK), 0).astype(F32)
        lane = lax.broadcasted_iota(jnp.int32, (CAP, 2 * TOK), 1)
        parts, columns = [], []
        for k in range(4):
            found = (ranks[k : k + 1] == slot) & (hits[k] > 0.5)
            for half in range(2):
                here = lane < TOK if half == 0 else lane >= TOK
                part = jnp.where(found & here, 1.0, 0.0)
                parts.append(part)
                columns.append(jnp.sum(part * scales[k], axis=1, keepdims=True))
        sel[pair] = jnp.concatenate(parts, axis=0).astype(BF16)
        gcol[pair] = jnp.broadcast_to(jnp.concatenate(columns, axis=0), (ROWS, 128))

    there = {}

    def dispatch(name, pair):
        buffer, staged, arrived = {"x": (gx, stx, ex), "c": (gc, stu, eu)}[name]
        for tile in range(0, WIDTH, 512):
            cols = pl.ds(tile, 512)
            rows = dot(sel[pair], buffer[2 * pair * TOK : 2 * (pair + 1) * TOK, cols], ROWS_COLS)
            if name == "c":
                rows = gcol[pair][:, 0:1] * rows
            rows = rows.astype(BF16)
            arrived[pair * ROWS : pair * ROWS + PAIR, cols] = rows[:PAIR]
            staged[pair * 3 * PAIR : (pair + 1) * 3 * PAIR, cols] = rows[PAIR:]
        there[name, pair] = new()
        for k in (2, 3, 1):
            send(
                "out",
                there[name, pair],
                staged.at[pl.ds((pair * 3 + k - 1) * PAIR, PAIR)],
                arrived.at[pl.ds((pair * 4 + k) * PAIR, PAIR)],
                plane[k],
            )

    returned = {}

    def from_others(ref, pair):
        return ref.at[pl.ds(pair * ROWS + PAIR, 3 * PAIR)]

    def rows_here(pair):
        arrive(there["x", pair], from_others(ex, pair))
        arrive(there["c", pair], from_others(eu, pair))

    def expert(pair):
        rows = slice(pair * ROWS, (pair + 1) * ROWS)
        for tile in range(0, FF, 256):
            cols = pl.ds(tile, 256)
            up_cols = pl.ds(FF + tile, 256)
            a = dot(ex[rows], wgu[:, cols], ROWS_COLS)
            b = dot(ex[rows], wgu[:, up_cols], ROWS_COLS)
            dh = dot(eu[rows], wdn[cols], LAST_LAST)
            s = jax.nn.sigmoid(a)
            active = a * s
            hb[rows, cols] = (active * b).astype(BF16)
            qb[rows, cols] = (dh * b * (s * (1.0 + a * (1.0 - s)))).astype(BF16)
            qb[rows, up_cols] = (dh * active).astype(BF16)
        for tile in range(0, WIDTH, 256):
            cols = pl.ds(tile, 256)
            value = dot(qb[rows], wgu[cols], LAST_LAST).astype(BF16)
            bk[rows, cols] = value
            rb[pair * ROWS : pair * ROWS + PAIR, cols] = value[:PAIR]

    def give_back(pair):
        returned[pair] = new()
        for k in (2, 3, 1):
            part = pl.ds((pair * 4 + k) * PAIR, PAIR)
            send("back", returned[pair], bk.at[part], rb.at[part], plane[k])

    def combine(pair):
        arrive(returned[pair], from_others(rb, pair))
        for tile in range(0, WIDTH, 512):
            cols = pl.ds(tile, 512)
            tgp[pair * 256 : (pair + 1) * 256, cols] = dot(
                sel[pair], rb[pair * ROWS : (pair + 1) * ROWS, cols], FIRST_FIRST
            )

    ways = ((0, 1, BEHIND), (1, -1, AHEAD))
    sums = {}

    def token_step(step, half):
        if step > 1:
            arrive(sums[step - 1, half], rz.at[step - 2, half])
        sums[step, half] = new()
        for index, way, order in ways:
            start, low = order[step] * TOK, index * 512 + half * 256
            term = tgp[start : start + TOK, low : low + 256]
            if step == 1:
                sz[half, index] = term.astype(BF16)
                source = sz.at[half, index]
            else:
                source = rz.at[step - 2, half, index]
                source[...] = (source[...].astype(F32) + term).astype(BF16)
            send("sums", sums[step, half], source, rz.at[step - 1, half, index], zdev(way))

    def token_last():
        for half in range(2):
            arrive(sums[7, half], rz.at[6, half])
            for index, _, _ in ways:
                low = index * 512 + half * 256
                total = tgp[OWN * TOK :, low : low + 256] + rz[6, half, index].astype(F32)
                tgb[:, low : low + 256] = total.astype(BF16)
        move(tgb, tg_out)

    parts = {"dn": (pdn, 0, PARTS[0]), "g0": (pgu, 0, PARTS[1]), "g1": (pgu, 32, PARTS[2])}
    kinds = list(parts)
    both = ("oth", "own")
    chain = {}

    def part_at(kind, side, delta):
        buffer, low, rows = parts[kind]
        return buffer.at[sides[side] * NY + lax.rem(y + delta + NY, NY), pl.ds(low, rows)]

    def grad_here(kind, side, number):
        received = ry[kinds.index(kind)].at[both.index(side), number - 1]
        if number == 4:
            received = received.at[0 if reach[side, 1] == 4 else 1]
        arrive(chain[kind, side, number], received)

    def grad_round(kind, side, number):
        received = ry[kinds.index(kind)].at[both.index(side)]
        if number > 1:
            grad_here(kind, side, number - 1)
        chain[kind, side, number] = new()
        for slot, way in ((0, 1), (1, -1)):
            left = reach[side, way] + 1 - number
            if left < 1:
                continue
            source = part_at(kind, side, way * left)
            if number > 1:
                term = source[...].astype(F32)
                source = received.at[number - 2, slot]
                source[...] = (source[...].astype(F32) + term).astype(BF16)
            target = received.at[number - 1, slot]
            send("grads", chain[kind, side, number], source, target, ydev(way))

    def grad_sum(kind, side):
        grad_here(kind, side, 4)
        total = part_at(kind, side, 0)[...].astype(F32)
        for slot, way in ((0, 1), (1, -1)):
            landed = ry[kinds.index(kind)][both.index(side), reach[side, way] - 1, slot]
            total = total + landed.astype(F32)
        return total

    results = {"dn": (dnb, dn_out, 0), "g0": (gub, gu_out, 0), "g1": (gub, gu_out, 32)}
    crossed, moved, spread, reached = {}, {}, {}, {}

    def grad_cross(kind):
        index = kinds.index(kind)
        tx[index][...] = grad_sum(kind, "oth").astype(BF16)
        crossed[kind] = new()
        send("swap", crossed[kind], tx[index], rx[index], other_side)

    def grad_swap(kind):
        index = kinds.index(kind)
        kept, _, start = results[kind]
        total = grad_sum(kind, "own")
        arrive(crossed[kind], rx[index])
        total = total + rx[index][...].astype(F32)
        kept[start : start + PARTS[index], :] = total
        total = total.astype(BF16)
        sl[index][...] = total
        for piece in range(NZ):
            cut[index][piece] = total[:, piece * 128 : (piece + 1) * 128]
        via[index][0] = cut[index][z]
        spread[kind], moved[kind] = new(), new()
        for r in range(1, NZ):
            source = cut[index].at[lax.rem(z + r, NZ)]
            send("pieces", spread[kind], source, via[index].at[r], zdev(r))
        for bit in (1, 0):
            send("swap", moved[kind], sl[index], rl[index].at[bit], plane[1 << bit])

    def grad_swap_on(kind):
        index = kinds.index(kind)
        arrive(spread[kind], via[index].at[pl.ds(1, NZ - 1)])
        reached[kind] = new()
        for r in range(NZ):
            taker = lax.rem(z + r, NZ)
            giver = lax.div(partner_ref[taker * 4 + c], 4)
            behind = lax.rem(z - giver + NZ, NZ)
            piece = via[index][0]
            for k in range(1, NZ):
                piece = jnp.where(behind == k, via[index][k], piece)
            if r == 0:
                whence[index][z] = piece
                continue
            onward[index][r] = piece
            send("pieces", reached[kind], onward[index].at[r], whence[index].at[z], zdev(r))

    def grad_last(kind):
        index = kinds.index(kind)
        kept, out, start = results[kind]
        mate = partner_ref[ei]
        arrive(moved[kind], rl[index])
        arrive(reached[kind], whence[index].at[pl.ds(1, NZ - 1)])
        value = kept[start : start + PARTS[index], :]
        for bit in range(2):
            value = jnp.where(mate == flip(ei, bit), rl[index][bit].astype(F32), value)
        pieces = [whence[index][piece].astype(F32) for piece in range(NZ)]
        value = jnp.where(lax.div(mate, 4) == z, value, jnp.concatenate(pieces, axis=1))
        kept[start : start + PARTS[index], :] = value
        place = pl.ds(start, PARTS[index])
        move(kept.at[place], out.at[place])

    early = 3 * ROWS

    def ahead_of_last():
        for tile in range(0, FF, 256):
            cols = pl.ds(tile, 256)
            adn[cols, :] = dot(hb[0:early, cols], eu[0:early], FIRST_FIRST)
        for tile in range(0, WIDTH, 256):
            cols = pl.ds(tile, 256)
            agu[cols, :] = dot(ex[0:early, cols], qb[0:early], FIRST_FIRST)

    def last_dn():
        for tile in range(0, FF, 256):
            cols = pl.ds(tile, 256)
            term = dot(hb[early:, cols], eu[early:], FIRST_FIRST)
            total = (adn[cols, :] + term).astype(BF16)
            pdn[tile // DN : (tile + 256) // DN] = total.reshape(256 // DN, DN, WIDTH)

    def last_gu():
        for tile in range(0, WIDTH, 256):
            cols = pl.ds(tile, 256)
            term = dot(ex[early:, cols], qb[early:], FIRST_FIRST)
            total = (agu[cols, :] + term).astype(BF16)
            pgu[tile // GU : (tile + 256) // GU] = total.reshape(256 // GU, GU, 2 * FF)

    arrive(across, one_slice)
    pass_weights("oth", 1)
    pass_weights("own", 2)
    pass_meta(2)
    pass_block("x", 2)
    choose(0)
    dispatch("x", 0)
    pass_weights("oth", 2)
    pass_block("c", 2)
    dispatch("c", 0)
    pass_weights("own", 3)
    pass_meta(3)
    pass_block("x", 3)
    choose(1)
    dispatch("x", 1)
    pass_weights("oth", 3)
    pass_block("c", 3)
    dispatch("c", 1)
    pass_weights("own", 4)
    pass_weights("oth", 4)
    pass_meta(4)
    pass_block("x", 4)
    choose(2)
    dispatch("x", 2)
    arrive(ring["m", 4], gm.at[OPPOSITE])
    choose(3)
    for copy in own_parts:
        copy.wait()
    pass_block("c", 4)
    dispatch("c", 2)
    last_weights("own")
    last_weights("oth")
    rows_here(0)
    expert(0)
    block_here("x", 4)
    dispatch("x", 3)
    rows_here(1)
    expert(1)
    block_here("c", 4)
    dispatch("c", 3)
    rows_here(2)
    expert(2)
    ahead_of_last()
    rows_here(3)
    give_back(0)
    expert(3)
    last_dn()
    grad_round("dn", "own", 1)
    last_gu()
    grad_round("g0", "oth", 1)
    give_back(1)
    grad_round("g1", "oth", 1)
    grad_round("dn", "oth", 1)
    combine(0)
    grad_round("dn", "own", 2)
    give_back(2)
    token_step(1, 1)
    grad_round("g1", "oth", 2)
    grad_round("g1", "own", 1)
    token_step(1, 0)
    combine(1)
    grad_round("dn", "oth", 2)
    token_step(2, 1)
    grad_round("dn", "own", 3)
    token_step(2, 0)
    grad_round("g0", "own", 1)
    give_back(3)
    combine(2)
    grad_round("dn", "oth", 3)
    grad_round("g1", "own", 2)
    token_step(3, 1)
    token_step(3, 0)
    grad_round("g0", "oth", 2)
    grad_round("g1", "oth", 3)
    grad_round("dn", "oth", 4)
    combine(3)
    token_step(4, 1)
    token_step(4, 0)
    grad_round("g0", "own", 2)
    grad_round("g0", "oth", 3)
    token_step(5, 1)
    grad_round("g1", "own", 3)
    grad_cross("dn")
    grad_round("g1", "oth", 4)
    grad_round("dn", "own", 4)
    token_step(5, 0)
    grad_round("g0", "own", 3)
    token_step(6, 1)
    grad_round("g0", "oth", 4)
    token_step(6, 0)
    grad_swap("dn")
    grad_cross("g1")
    token_step(7, 1)
    grad_round("g1", "own", 4)
    grad_round("g0", "own", 4)
    grad_cross("g0")
    token_step(7, 0)
    grad_swap("g1")
    grad_swap("g0")
    grad_swap_on("dn")
    token_last()
    grad_swap_on("g1")
    grad_swap_on("g0")
    grad_last("dn")
    grad_last("g1")
    grad_last("g0")
    for copy in local[len(own_parts) :]:
        copy.wait()
    for group, sources in sent.items():
        size = sum(math.prod(source.shape) for source in sources)
        if group == "meta":
            whole_group = gm.at[pl.ds(0, size // (8 * TOK))]
        elif group == "pieces":
            whole_group = hb.at[pl.ds(0, size // FF)]
        else:
            whole_group = agu.at[pl.ds(0, size // (2 * WIDTH))]
        pltpu.make_async_remote_copy(
            src_ref=whole_group,
            dst_ref=whole_group,
            send_sem=ssem.at[GROUPS.index(group)],
            recv_sem=rsem.at[0],
            device_id=other_side,
            device_id_type=MESH,
        ).wait_send()
    assert len(receives) <= RECEIVES


def hand_on(*refs):
    count = len(refs) // 2
    sources, results, sem = refs[:count], refs[count:-1], refs[-1]
    copies = []
    for index in range(count):
        target = results[index] if index == 0 else results[index].at[0]
        copies.append(pltpu.make_async_copy(sources[index], target, sem.at[index]))
        copies[index].start()
    for copy in copies:
        copy.wait()


def body(tokens, cotangent, gates, expert_ids, placement, partner, w_gate_up, w_down):
    def vmem(*shape, dtype=BF16):
        return pltpu.VMEM(shape, dtype)

    slots = 4 * ROWS
    scratch = [
        vmem(NZ * TOK, WIDTH),
        vmem(NZ * TOK, WIDTH),
        vmem(NZ, 8, TOK, dtype=F32),
        vmem(2 * TOK, 2 * TOK),
        vmem(4, ROWS, 2 * TOK),
        vmem(4, ROWS, 128, dtype=F32),
        vmem(12 * PAIR, WIDTH),
        vmem(12 * PAIR, WIDTH),
        vmem(slots, WIDTH),
        vmem(slots, WIDTH),
        vmem(WIDTH, 2 * FF),
        vmem(FF, WIDTH),
        vmem(slots, FF),
        vmem(slots, 2 * FF),
        vmem(slots, WIDTH),
        vmem(slots, WIDTH),
        vmem(NZ * TOK, WIDTH, dtype=F32),
        vmem(2, 2, TOK, 256),
        vmem(7, 2, 2, TOK, 256),
        vmem(WIDTH, 2 * FF, dtype=F32),
        vmem(FF, WIDTH, dtype=F32),
        vmem(16, GU, 2 * FF),
        vmem(16, DN, WIDTH),
        [vmem(2, 4, 2, rows, WIDTH) for rows in PARTS],
        [vmem(rows, WIDTH) for rows in PARTS],
        [vmem(rows, WIDTH) for rows in PARTS],
        [vmem(rows, WIDTH) for rows in PARTS],
        [vmem(2, rows, WIDTH) for rows in PARTS],
        [vmem(NZ, rows, 128) for rows in PARTS],
        [vmem(NZ, rows, 128) for rows in PARTS],
        [vmem(NZ, rows, 128) for rows in PARTS],
        [vmem(NZ, rows, 128) for rows in PARTS],
        vmem(TOK, WIDTH),
        vmem(GU, 2 * FF, dtype=F32),
        vmem(DN, WIDTH, dtype=F32),
        pltpu.SemaphoreType.DMA((len(GROUPS),)),
        pltpu.SemaphoreType.DMA((RECEIVES,)),
        pltpu.SemaphoreType.DMA((8,)),
    ]
    in_vmem = pl.BlockSpec(memory_space=pltpu.VMEM)
    in_smem = pl.BlockSpec(memory_space=pltpu.SMEM)
    anywhere = pl.BlockSpec(memory_space=pl.ANY)
    results = pl.pallas_call(
        kernel,
        out_shape=(
            pltpu.VMEM((TOK, WIDTH), BF16),
            pltpu.VMEM((GU, 2 * FF), F32),
            pltpu.VMEM((DN, WIDTH), F32),
        ),
        in_specs=[in_vmem] * 2 + [anywhere] * 4 + [in_smem] * 2,
        out_specs=(anywhere,) * 3,
        scratch_shapes=scratch,
        compiler_params=pltpu.CompilerParams(
            collective_id=0, has_side_effects=True, vmem_limit_bytes=58 * 1024 * 1024
        ),
    )(expert_ids.T, gates.T, tokens, cotangent, w_gate_up, w_down, placement, partner)
    return pl.pallas_call(
        hand_on,
        out_shape=(
            jax.ShapeDtypeStruct((TOK, WIDTH), BF16),
            jax.ShapeDtypeStruct((1, GU, 2 * FF), F32),
            jax.ShapeDtypeStruct((1, DN, WIDTH), F32),
        ),
        in_specs=[in_vmem] * 3,
        out_specs=(anywhere,) * 3,
        scratch_shapes=[pltpu.SemaphoreType.DMA((3,))],
        compiler_params=pltpu.CompilerParams(vmem_limit_bytes=1024 * 1024),
    )(*results)


def solution(mesh):
    return jax.shard_map(
        body,
        mesh=mesh,
        in_specs=(
            P(("dp", "expert"), None),
            P(("dp", "expert"), None),
            P(("dp", "expert"), None),
            P(("dp", "expert"), None),
            P(),
            P(),
            P("expert", "dp", None),
            P("expert", "dp", None),
        ),
        out_specs=(P(("dp", "expert"), None), P("expert", "dp", None), P("expert", "dp", None)),
        check_vma=False,
    )
```

```python
import math

import jax
import jax.numpy as jnp
from jax import lax
from jax.experimental import pallas as pl
from jax.experimental.pallas import tpu as pltpu
from jax.sharding import PartitionSpec as P

MESH = pl.DeviceIdType.MESH
BF16 = jnp.bfloat16
F32 = jnp.float32

NZ = 8
NY = 8
CAP = 24
PAIR = 2 * CAP
ROWS = 4 * PAIR
TOK = 128
WIDTH = 1024
FF = 512
GU = 64
DN = 32
PARTS = (32, 32, 32)
RECEIVES = 89
GROUPS = ("weights", "meta", "ring", "out", "back", "sums", "grads", "swap", "pieces")

BEHIND = {1: 0, 2: 2, 3: 4, 4: 6, 5: 5, 6: 3, 7: 1}
AHEAD = {1: 1, 2: 3, 3: 5, 4: 6, 5: 4, 6: 2, 7: 0}
OPPOSITE, OWN = 6, 7


def flip(value, bit):
    size = 1 << bit
    return value + size - 2 * size * (lax.rem(lax.div(value, size), 2))


def dot(a, b, dims):
    return lax.dot_general(a, b, (dims, ((), ())), preferred_element_type=F32)


ROWS_COLS = ((1,), (0,))
LAST_LAST = ((1,), (1,))
FIRST_FIRST = ((0,), (0,))


def kernel(
    ids_ref, gates_ref, tok_ref, cot_ref, gu_ref, dn_ref, placement_ref, partner_ref,
    tg_out, gu_out, dn_out,
    gx, gc, gm, tri, sel, gcol, stx, stu, ex, eu, wgu, wdn, hb, qb, bk, rb,
    tgp, sz, rz, agu, adn, pgu, pdn, ry, tx, rx, sl, rl, cut, via, onward, whence,
    ssem, rsem, lsem,
):
    dpi = lax.axis_index("dp")
    ei = lax.axis_index("expert")
    xl, y = lax.div(dpi, NY), lax.rem(dpi, NY)
    z, c = lax.div(ei, 4), lax.rem(ei, 4)

    def ydev(delta):
        return (xl * NY + lax.rem(y + delta + NY, NY), ei)

    def zdev(delta):
        return (dpi, lax.rem(z + delta + NZ, NZ) * 4 + c)

    column = [c, flip(c, 0), flip(c, 1), flip(flip(c, 0), 1)]
    plane = [(dpi, z * 4 + q) for q in column]
    other_side = ((1 - xl) * NY + y, ei)

    barrier = pltpu.get_barrier_semaphore()
    peers = [zdev(r) for r in range(1, NZ)] + plane[1:] + [ydev(1), ydev(-1), other_side]
    for peer in peers:
        pl.semaphore_signal(barrier, inc=1, device_id=peer, device_id_type=MESH)
    pl.semaphore_wait(barrier, len(peers))

    sent = {group: [] for group in GROUPS}
    receives = []

    local = []

    def move(src, dst):
        copy = pltpu.make_async_copy(src, dst, lsem.at[len(local)])
        copy.start()
        local.append(copy)
        return copy

    def new():
        receives.append(len(receives))
        return receives[-1]

    def send(group, receive, src, dst, device):
        copy = pltpu.make_async_remote_copy(
            src_ref=src,
            dst_ref=dst,
            send_sem=ssem.at[GROUPS.index(group)],
            recv_sem=rsem.at[receive],
            device_id=device,
            device_id_type=MESH,
        )
        copy.start()
        sent[group].append(src)

    def arrive(receive, ref):
        pltpu.make_async_remote_copy(
            src_ref=ref,
            dst_ref=ref,
            send_sem=ssem.at[0],
            recv_sem=rsem.at[receive],
            device_id=other_side,
            device_id_type=MESH,
        ).wait_recv()

    def slice_at(ref, rows, side, delta):
        owner = side * NY + lax.rem(y + delta + NY, NY)
        return ref.at[pl.ds(pl.multiple_of(owner * rows, rows), rows)]

    sides = {"own": xl, "oth": 1 - xl}
    whole = {"gu": (wgu, GU, gu_ref.at[0]), "dn": (wdn, DN, dn_ref.at[0])}
    reach = {("own", 1): 4, ("own", -1): 3, ("oth", 1): 3, ("oth", -1): 4}
    coming = {}
    one_slice = wgu.at[pl.ds(0, GU + DN)]

    def pass_weights(side, hop):
        for way in (1, -1):
            if hop > reach[side, way]:
                continue
            if hop > 1:
                arrive(coming[side, way, hop - 1], one_slice)
            coming[side, way, hop] = new()
            for buffer, rows, mine in whole.values():
                target = slice_at(buffer, rows, sides[side], -way * (hop - 1))
                source = mine if hop == 1 and side == "own" else target
                send("weights", coming[side, way, hop], source, target, ydev(way))

    def last_weights(side):
        for way in (1, -1):
            arrive(coming[side, way, reach[side, way]], one_slice)

    across = new()
    for buffer, rows, mine in whole.values():
        send("weights", across, mine, slice_at(buffer, rows, xl, 0), other_side)
    pass_weights("own", 1)

    def block(ref, index):
        return ref.at[pl.ds(index * TOK, TOK)]

    ring = {}

    def pass_meta(hop):
        if hop > 1:
            arrive(ring["m", hop - 1], gm.at[pl.ds(2 * hop - 4, 2)])
        ring["m", hop] = new()
        for way, order in ((1, BEHIND), (-1, AHEAD)):
            if hop > 3 and way < 0:
                continue
            source = gm.at[OWN if hop == 1 else order[hop - 1]]
            send("meta", ring["m", hop], source, gm.at[order[hop]], zdev(way))

    def block_here(name, hop):
        buffer = gx if name == "x" else gc
        arrive(ring[name, hop], buffer.at[pl.ds(2 * (hop - 1) * TOK, TOK if hop == 4 else 2 * TOK)])

    def pass_block(name, hop):
        mine, buffer = {"x": (tok_ref, gx), "c": (cot_ref, gc)}[name]
        if hop > 1:
            block_here(name, hop - 1)
        half = TOK // 2
        ring[name, hop] = new()
        for way, order in ((1, BEHIND), (-1, AHEAD)):
            source = mine if hop == 1 else block(buffer, order[hop - 1])
            target = block(buffer, order[hop])
            if hop == 4:
                part = pl.ds(0 if way > 0 else half, half)
                source, target = source.at[part], target.at[part]
            send("ring", ring[name, hop], source, target, zdev(way))

    ids = ids_ref[...]
    holder = jnp.zeros(ids.shape, F32)
    for e in range(32):
        holder = jnp.where(ids == e, partner_ref[placement_ref[e]].astype(F32), holder)
    gm[OWN, 0:4, :] = holder
    gm[OWN, 4:8, :] = gates_ref[...]
    pass_meta(1)
    pass_block("x", 1)
    pass_block("c", 1)
    own_parts = [move(tok_ref, block(gx, OWN)), move(cot_ref, block(gc, OWN))]
    for buffer, rows, mine in whole.values():
        own_parts.append(move(mine, slice_at(buffer, rows, xl, 0)))

    before = lax.broadcasted_iota(jnp.int32, (2 * TOK, 2 * TOK), 0)
    after = lax.broadcasted_iota(jnp.int32, (2 * TOK, 2 * TOK), 1)
    same_block = lax.div(before, TOK) == lax.div(after, TOK)
    tri[...] = jnp.where(same_block & (before < after), 1.0, 0.0).astype(BF16)

    def choose(pair):
        both = jnp.concatenate([gm[2 * pair], gm[2 * pair + 1]], axis=1)
        named, weight = both[0:4], both[4:8]
        hits, scales = [], []
        for q in column:
            hit = jnp.where(named == (z * 4 + q).astype(F32), 1.0, 0.0)
            hits.append(jnp.sum(hit, axis=0, keepdims=True))
            scales.append(jnp.sum(hit * weight, axis=0, keepdims=True))
        marks = jnp.concatenate(hits + [jnp.zeros((12, 2 * TOK), F32)], axis=0)
        ranks = dot(marks.astype(BF16), tri[...], ROWS_COLS)
        slot = lax.broadcasted_iota(jnp.int32, (CAP, 2 * TOK), 0).astype(F32)
        lane = lax.broadcasted_iota(jnp.int32, (CAP, 2 * TOK), 1)
        parts, columns = [], []
        for k in range(4):
            found = (ranks[k : k + 1] == slot) & (hits[k] > 0.5)
            for half in range(2):
                here = lane < TOK if half == 0 else lane >= TOK
                part = jnp.where(found & here, 1.0, 0.0)
                parts.append(part)
                columns.append(jnp.sum(part * scales[k], axis=1, keepdims=True))
        sel[pair] = jnp.concatenate(parts, axis=0).astype(BF16)
        gcol[pair] = jnp.broadcast_to(jnp.concatenate(columns, axis=0), (ROWS, 128))

    there = {}

    def dispatch(name, pair):
        buffer, staged, arrived = {"x": (gx, stx, ex), "c": (gc, stu, eu)}[name]
        for tile in range(0, WIDTH, 512):
            cols = pl.ds(tile, 512)
            rows = dot(sel[pair], buffer[2 * pair * TOK : 2 * (pair + 1) * TOK, cols], ROWS_COLS)
            if name == "c":
                rows = gcol[pair][:, 0:1] * rows
            rows = rows.astype(BF16)
            arrived[pair * ROWS : pair * ROWS + PAIR, cols] = rows[:PAIR]
            staged[pair * 3 * PAIR : (pair + 1) * 3 * PAIR, cols] = rows[PAIR:]
        there[name, pair] = new()
        for k in (2, 3, 1):
            send(
                "out",
                there[name, pair],
                staged.at[pl.ds((pair * 3 + k - 1) * PAIR, PAIR)],
                arrived.at[pl.ds((pair * 4 + k) * PAIR, PAIR)],
                plane[k],
            )

    returned = {}

    def from_others(ref, pair):
        return ref.at[pl.ds(pair * ROWS + PAIR, 3 * PAIR)]

    def rows_here(pair):
        arrive(there["x", pair], from_others(ex, pair))
        arrive(there["c", pair], from_others(eu, pair))

    def expert(pair):
        rows = slice(pair * ROWS, (pair + 1) * ROWS)
        for tile in range(0, FF, 256):
            cols = pl.ds(tile, 256)
            up_cols = pl.ds(FF + tile, 256)
            a = dot(ex[rows], wgu[:, cols], ROWS_COLS)
            b = dot(ex[rows], wgu[:, up_cols], ROWS_COLS)
            dh = dot(eu[rows], wdn[cols], LAST_LAST)
            s = jax.nn.sigmoid(a)
            active = a * s
            hb[rows, cols] = (active * b).astype(BF16)
            qb[rows, cols] = (dh * b * (s * (1.0 + a * (1.0 - s)))).astype(BF16)
            qb[rows, up_cols] = (dh * active).astype(BF16)

    def expert_back(pair):
        rows = slice(pair * ROWS, (pair + 1) * ROWS)
        for tile in range(0, WIDTH, 256):
            cols = pl.ds(tile, 256)
            value = dot(qb[rows], wgu[cols], LAST_LAST).astype(BF16)
            bk[rows, cols] = value
            rb[pair * ROWS : pair * ROWS + PAIR, cols] = value[:PAIR]

    def give_back(pair):
        returned[pair] = new()
        for k in (2, 3, 1):
            part = pl.ds((pair * 4 + k) * PAIR, PAIR)
            send("back", returned[pair], bk.at[part], rb.at[part], plane[k])

    def combine(pair):
        arrive(returned[pair], from_others(rb, pair))
        for tile in range(0, WIDTH, 512):
            cols = pl.ds(tile, 512)
            tgp[pair * 256 : (pair + 1) * 256, cols] = dot(
                sel[pair], rb[pair * ROWS : (pair + 1) * ROWS, cols], FIRST_FIRST
            )

    ways = ((0, 1, BEHIND), (1, -1, AHEAD))
    sums = {}

    def token_step(step, half):
        if step > 1:
            arrive(sums[step - 1, half], rz.at[step - 2, half])
        sums[step, half] = new()
        for index, way, order in ways:
            start, low = order[step] * TOK, index * 512 + half * 256
            term = tgp[start : start + TOK, low : low + 256]
            if step == 1:
                sz[half, index] = term.astype(BF16)
                source = sz.at[half, index]
            else:
                source = rz.at[step - 2, half, index]
                source[...] = (source[...].astype(F32) + term).astype(BF16)
            send("sums", sums[step, half], source, rz.at[step - 1, half, index], zdev(way))

    def token_last():
        for half in range(2):
            arrive(sums[7, half], rz.at[6, half])
            for index, _, _ in ways:
                low = index * 512 + half * 256
                total = tgp[OWN * TOK :, low : low + 256] + rz[6, half, index].astype(F32)
                tg_out[:, low : low + 256] = total.astype(BF16)

    parts = {"dn": (pdn, 0, PARTS[0]), "g0": (pgu, 0, PARTS[1]), "g1": (pgu, 32, PARTS[2])}
    kinds = list(parts)
    both = ("oth", "own")
    chain = {}

    def part_at(kind, side, delta):
        buffer, low, rows = parts[kind]
        return buffer.at[sides[side] * NY + lax.rem(y + delta + NY, NY), pl.ds(low, rows)]

    def grad_here(kind, side, number):
        received = ry[kinds.index(kind)].at[both.index(side), number - 1]
        if number == 4:
            received = received.at[0 if reach[side, 1] == 4 else 1]
        arrive(chain[kind, side, number], received)

    def grad_round(kind, side, number):
        received = ry[kinds.index(kind)].at[both.index(side)]
        if number > 1:
            grad_here(kind, side, number - 1)
        chain[kind, side, number] = new()
        for slot, way in ((0, 1), (1, -1)):
            left = reach[side, way] + 1 - number
            if left < 1:
                continue
            source = part_at(kind, side, way * left)
            if number > 1:
                term = source[...].astype(F32)
                source = received.at[number - 2, slot]
                source[...] = (source[...].astype(F32) + term).astype(BF16)
            target = received.at[number - 1, slot]
            send("grads", chain[kind, side, number], source, target, ydev(way))

    def grad_sum(kind, side):
        grad_here(kind, side, 4)
        total = part_at(kind, side, 0)[...].astype(F32)
        for slot, way in ((0, 1), (1, -1)):
            landed = ry[kinds.index(kind)][both.index(side), reach[side, way] - 1, slot]
            total = total + landed.astype(F32)
        return total

    results = {"dn": (dn_out, 0), "g0": (gu_out, 0), "g1": (gu_out, 32)}
    crossed, moved, spread, reached = {}, {}, {}, {}

    def grad_cross(kind):
        index = kinds.index(kind)
        tx[index][...] = grad_sum(kind, "oth").astype(BF16)
        crossed[kind] = new()
        send("swap", crossed[kind], tx[index], rx[index], other_side)

    def grad_swap(kind):
        index = kinds.index(kind)
        kept, start = results[kind]
        total = grad_sum(kind, "own")
        arrive(crossed[kind], rx[index])
        total = total + rx[index][...].astype(F32)
        kept[start : start + PARTS[index], :] = total
        total = total.astype(BF16)
        sl[index][...] = total
        for piece in range(NZ):
            cut[index][piece] = total[:, piece * 128 : (piece + 1) * 128]
        via[index][0] = cut[index][z]
        spread[kind], moved[kind] = new(), new()
        for r in range(1, NZ):
            source = cut[index].at[lax.rem(z + r, NZ)]
            send("pieces", spread[kind], source, via[index].at[r], zdev(r))
        for bit in (1, 0):
            send("swap", moved[kind], sl[index], rl[index].at[bit], plane[1 << bit])

    def grad_swap_on(kind):
        index = kinds.index(kind)
        arrive(spread[kind], via[index].at[pl.ds(1, NZ - 1)])
        reached[kind] = new()
        for r in range(NZ):
            taker = lax.rem(z + r, NZ)
            giver = lax.div(partner_ref[taker * 4 + c], 4)
            behind = lax.rem(z - giver + NZ, NZ)
            piece = via[index][0]
            for k in range(1, NZ):
                piece = jnp.where(behind == k, via[index][k], piece)
            if r == 0:
                whence[index][z] = piece
                continue
            onward[index][r] = piece
            send("pieces", reached[kind], onward[index].at[r], whence[index].at[z], zdev(r))

    def grad_last(kind):
        index = kinds.index(kind)
        kept, start = results[kind]
        mate = partner_ref[ei]
        arrive(moved[kind], rl[index])
        arrive(reached[kind], whence[index].at[pl.ds(1, NZ - 1)])
        value = kept[start : start + PARTS[index], :]
        for bit in range(2):
            value = jnp.where(mate == flip(ei, bit), rl[index][bit].astype(F32), value)
        pieces = [whence[index][piece].astype(F32) for piece in range(NZ)]
        value = jnp.where(lax.div(mate, 4) == z, value, jnp.concatenate(pieces, axis=1))
        kept[start : start + PARTS[index], :] = value

    early = 3 * ROWS

    def ahead_of_last():
        for tile in range(0, FF, 256):
            cols = pl.ds(tile, 256)
            adn[cols, :] = dot(hb[0:early, cols], eu[0:early], FIRST_FIRST)
        for tile in range(0, WIDTH, 256):
            cols = pl.ds(tile, 256)
            agu[cols, :] = dot(ex[0:early, cols], qb[0:early], FIRST_FIRST)

    def last_dn():
        for tile in range(0, FF, 256):
            cols = pl.ds(tile, 256)
            term = dot(hb[early:, cols], eu[early:], FIRST_FIRST)
            total = (adn[cols, :] + term).astype(BF16)
            pdn[tile // DN : (tile + 256) // DN] = total.reshape(256 // DN, DN, WIDTH)

    def last_gu():
        for tile in range(0, WIDTH, 256):
            cols = pl.ds(tile, 256)
            term = dot(ex[early:, cols], qb[early:], FIRST_FIRST)
            total = (agu[cols, :] + term).astype(BF16)
            pgu[tile // GU : (tile + 256) // GU] = total.reshape(256 // GU, GU, 2 * FF)

    arrive(across, one_slice)
    pass_weights("oth", 1)
    pass_weights("own", 2)
    pass_meta(2)
    pass_block("x", 2)
    choose(0)
    dispatch("x", 0)
    pass_weights("oth", 2)
    pass_block("c", 2)
    dispatch("c", 0)
    pass_weights("own", 3)
    pass_meta(3)
    pass_block("x", 3)
    choose(1)
    dispatch("x", 1)
    pass_weights("oth", 3)
    pass_block("c", 3)
    dispatch("c", 1)
    pass_weights("own", 4)
    pass_weights("oth", 4)
    pass_meta(4)
    pass_block("x", 4)
    choose(2)
    dispatch("x", 2)
    arrive(ring["m", 4], gm.at[OPPOSITE])
    choose(3)
    for copy in own_parts:
        copy.wait()
    pass_block("c", 4)
    dispatch("c", 2)
    last_weights("own")
    last_weights("oth")
    rows_here(0)
    expert(0)
    expert_back(0)
    block_here("x", 4)
    dispatch("x", 3)
    rows_here(1)
    expert(1)
    expert_back(1)
    block_here("c", 4)
    dispatch("c", 3)
    rows_here(2)
    expert(2)
    expert_back(2)
    ahead_of_last()
    rows_here(3)
    give_back(0)
    expert(3)
    last_dn()
    grad_round("dn", "own", 1)
    last_gu()
    grad_round("g0", "oth", 1)
    give_back(1)
    grad_round("g1", "oth", 1)
    grad_round("dn", "oth", 1)
    combine(0)
    grad_round("dn", "own", 2)
    give_back(2)
    token_step(1, 1)
    grad_round("g1", "oth", 2)
    grad_round("g1", "own", 1)
    token_step(1, 0)
    combine(1)
    grad_round("dn", "oth", 2)
    token_step(2, 1)
    grad_round("dn", "own", 3)
    token_step(2, 0)
    grad_round("g0", "own", 1)
    expert_back(3)
    give_back(3)
    combine(2)
    grad_round("dn", "oth", 3)
    grad_round("g1", "own", 2)
    token_step(3, 1)
    token_step(3, 0)
    grad_round("g0", "oth", 2)
    grad_round("g1", "oth", 3)
    grad_round("dn", "oth", 4)
    combine(3)
    token_step(4, 1)
    token_step(4, 0)
    grad_round("g0", "own", 2)
    grad_round("g0", "oth", 3)
    token_step(5, 1)
    grad_round("g1", "own", 3)
    grad_cross("dn")
    grad_round("g1", "oth", 4)
    grad_round("dn", "own", 4)
    token_step(5, 0)
    grad_round("g0", "own", 3)
    token_step(6, 1)
    grad_round("g0", "oth", 4)
    token_step(6, 0)
    grad_swap("dn")
    grad_cross("g1")
    token_step(7, 1)
    grad_round("g1", "own", 4)
    grad_round("g0", "own", 4)
    grad_cross("g0")
    token_step(7, 0)
    grad_swap("g1")
    grad_swap("g0")
    grad_swap_on("dn")
    token_last()
    grad_swap_on("g1")
    grad_swap_on("g0")
    grad_last("dn")
    grad_last("g1")
    grad_last("g0")
    for group, sources in sent.items():
        size = sum(math.prod(source.shape) for source in sources)
        if group == "meta":
            whole_group = gm.at[pl.ds(0, size // (8 * TOK))]
        elif group == "pieces":
            whole_group = hb.at[pl.ds(0, size // FF)]
        else:
            whole_group = agu.at[pl.ds(0, size // (2 * WIDTH))]
        pltpu.make_async_remote_copy(
            src_ref=whole_group,
            dst_ref=whole_group,
            send_sem=ssem.at[GROUPS.index(group)],
            recv_sem=rsem.at[0],
            device_id=other_side,
            device_id_type=MESH,
        ).wait_send()
    assert len(receives) <= RECEIVES


def hand_on(*refs):
    count = len(refs) // 2
    sources, results, sem = refs[:count], refs[count:-1], refs[-1]
    copies = []
    for index in range(count):
        target = results[index] if index == 0 else results[index].at[0]
        copies.append(pltpu.make_async_copy(sources[index], target, sem.at[index]))
        copies[index].start()
    for copy in copies:
        copy.wait()


def body(tokens, cotangent, gates, expert_ids, placement, partner, w_gate_up, w_down):
    def vmem(*shape, dtype=BF16):
        return pltpu.VMEM(shape, dtype)

    slots = 4 * ROWS
    scratch = [
        vmem(NZ * TOK, WIDTH),
        vmem(NZ * TOK, WIDTH),
        vmem(NZ, 8, TOK, dtype=F32),
        vmem(2 * TOK, 2 * TOK),
        vmem(4, ROWS, 2 * TOK),
        vmem(4, ROWS, 128, dtype=F32),
        vmem(12 * PAIR, WIDTH),
        vmem(12 * PAIR, WIDTH),
        vmem(slots, WIDTH),
        vmem(slots, WIDTH),
        vmem(WIDTH, 2 * FF),
        vmem(FF, WIDTH),
        vmem(slots, FF),
        vmem(slots, 2 * FF),
        vmem(slots, WIDTH),
        vmem(slots, WIDTH),
        vmem(NZ * TOK, WIDTH, dtype=F32),
        vmem(2, 2, TOK, 256),
        vmem(7, 2, 2, TOK, 256),
        vmem(WIDTH, 2 * FF, dtype=F32),
        vmem(FF, WIDTH, dtype=F32),
        vmem(16, GU, 2 * FF),
        vmem(16, DN, WIDTH),
        [vmem(2, 4, 2, rows, WIDTH) for rows in PARTS],
        [vmem(rows, WIDTH) for rows in PARTS],
        [vmem(rows, WIDTH) for rows in PARTS],
        [vmem(rows, WIDTH) for rows in PARTS],
        [vmem(2, rows, WIDTH) for rows in PARTS],
        [vmem(NZ, rows, 128) for rows in PARTS],
        [vmem(NZ, rows, 128) for rows in PARTS],
        [vmem(NZ, rows, 128) for rows in PARTS],
        [vmem(NZ, rows, 128) for rows in PARTS],
        pltpu.SemaphoreType.DMA((len(GROUPS),)),
        pltpu.SemaphoreType.DMA((RECEIVES,)),
        pltpu.SemaphoreType.DMA((4,)),
    ]
    in_vmem = pl.BlockSpec(memory_space=pltpu.VMEM)
    in_smem = pl.BlockSpec(memory_space=pltpu.SMEM)
    anywhere = pl.BlockSpec(memory_space=pl.ANY)
    results = pl.pallas_call(
        kernel,
        out_shape=(
            pltpu.VMEM((TOK, WIDTH), BF16),
            pltpu.VMEM((GU, 2 * FF), F32),
            pltpu.VMEM((DN, WIDTH), F32),
        ),
        in_specs=[in_vmem] * 2 + [anywhere] * 4 + [in_smem] * 2,
        out_specs=(in_vmem,) * 3,
        scratch_shapes=scratch,
        compiler_params=pltpu.CompilerParams(
            collective_id=0, has_side_effects=True, vmem_limit_bytes=58 * 1024 * 1024
        ),
    )(expert_ids.T, gates.T, tokens, cotangent, w_gate_up, w_down, placement, partner)
    return pl.pallas_call(
        hand_on,
        out_shape=(
            jax.ShapeDtypeStruct((TOK, WIDTH), BF16),
            jax.ShapeDtypeStruct((1, GU, 2 * FF), F32),
            jax.ShapeDtypeStruct((1, DN, WIDTH), F32),
        ),
        in_specs=[in_vmem] * 3,
        out_specs=(anywhere,) * 3,
        scratch_shapes=[pltpu.SemaphoreType.DMA((3,))],
        compiler_params=pltpu.CompilerParams(vmem_limit_bytes=1024 * 1024),
    )(*results)


def solution(mesh):
    return jax.shard_map(
        body,
        mesh=mesh,
        in_specs=(
            P(("dp", "expert"), None),
            P(("dp", "expert"), None),
            P(("dp", "expert"), None),
            P(("dp", "expert"), None),
            P(),
            P(),
            P("expert", "dp", None),
            P("expert", "dp", None),
        ),
        out_specs=(P(("dp", "expert"), None), P("expert", "dp", None), P("expert", "dp", None)),
        check_vma=False,
    )
```

```python
import math

import jax
import jax.numpy as jnp
from jax import lax
from jax.experimental import pallas as pl
from jax.experimental.pallas import tpu as pltpu
from jax.sharding import PartitionSpec as P

MESH = pl.DeviceIdType.MESH
BF16 = jnp.bfloat16
F32 = jnp.float32

NZ = 8
NY = 8
CAP = 24
PAIR = 2 * CAP
ROWS = 4 * PAIR
TOK = 128
WIDTH = 1024
FF = 512
GU = 64
DN = 32
PARTS = (32, 32, 32)
RECEIVES = 89
GROUPS = ("weights", "meta", "ring", "out", "back", "sums", "grads", "swap", "pieces")

BEHIND = {1: 0, 2: 2, 3: 4, 4: 6, 5: 5, 6: 3, 7: 1}
AHEAD = {1: 1, 2: 3, 3: 5, 4: 6, 5: 4, 6: 2, 7: 0}
OPPOSITE, OWN = 6, 7


def flip(value, bit):
    size = 1 << bit
    return value + size - 2 * size * (lax.rem(lax.div(value, size), 2))


def dot(a, b, dims):
    return lax.dot_general(a, b, (dims, ((), ())), preferred_element_type=F32)


ROWS_COLS = ((1,), (0,))
LAST_LAST = ((1,), (1,))
FIRST_FIRST = ((0,), (0,))


def kernel(
    ids_ref, gates_ref, tok_ref, cot_ref, gu_ref, dn_ref, placement_ref, partner_ref,
    tg_out, gu_out, dn_out,
    gx, gc, gm, tri, sel, gcol, stx, stu, ex, eu, wgu, wdn, hb, qb, bk, rb,
    tgp, sz, rz, agu, adn, pgu, pdn, ry, tx, rx, sl, rl, cut, via, onward, whence,
    ssem, rsem, lsem,
):
    dpi = lax.axis_index("dp")
    ei = lax.axis_index("expert")
    xl, y = lax.div(dpi, NY), lax.rem(dpi, NY)
    z, c = lax.div(ei, 4), lax.rem(ei, 4)

    def ydev(delta):
        return (xl * NY + lax.rem(y + delta + NY, NY), ei)

    def zdev(delta):
        return (dpi, lax.rem(z + delta + NZ, NZ) * 4 + c)

    column = [c, flip(c, 0), flip(c, 1), flip(flip(c, 0), 1)]
    plane = [(dpi, z * 4 + q) for q in column]
    other_side = ((1 - xl) * NY + y, ei)

    barrier = pltpu.get_barrier_semaphore()
    peers = [zdev(r) for r in range(1, NZ)] + plane[1:] + [ydev(1), ydev(-1), other_side]
    for peer in peers:
        pl.semaphore_signal(barrier, inc=1, device_id=peer, device_id_type=MESH)
    pl.semaphore_wait(barrier, len(peers))

    sent = {group: [] for group in GROUPS}
    receives = []

    local = []

    def move(src, dst):
        copy = pltpu.make_async_copy(src, dst, lsem.at[len(local)])
        copy.start()
        local.append(copy)
        return copy

    def new():
        receives.append(len(receives))
        return receives[-1]

    def send(group, receive, src, dst, device):
        copy = pltpu.make_async_remote_copy(
            src_ref=src,
            dst_ref=dst,
            send_sem=ssem.at[GROUPS.index(group)],
            recv_sem=rsem.at[receive],
            device_id=device,
            device_id_type=MESH,
        )
        copy.start()
        sent[group].append(src)

    def arrive(receive, ref):
        pltpu.make_async_remote_copy(
            src_ref=ref,
            dst_ref=ref,
            send_sem=ssem.at[0],
            recv_sem=rsem.at[receive],
            device_id=other_side,
            device_id_type=MESH,
        ).wait_recv()

    def slice_at(ref, rows, side, delta):
        owner = side * NY + lax.rem(y + delta + NY, NY)
        return ref.at[pl.ds(pl.multiple_of(owner * rows, rows), rows)]

    sides = {"own": xl, "oth": 1 - xl}
    whole = {"gu": (wgu, GU, gu_ref.at[0]), "dn": (wdn, DN, dn_ref.at[0])}
    reach = {("own", 1): 4, ("own", -1): 3, ("oth", 1): 3, ("oth", -1): 4}
    coming = {}
    one_slice = wgu.at[pl.ds(0, GU + DN)]

    def pass_weights(side, hop):
        for way in (1, -1):
            if hop > reach[side, way]:
                continue
            if hop > 1:
                arrive(coming[side, way, hop - 1], one_slice)
            coming[side, way, hop] = new()
            for buffer, rows, mine in whole.values():
                target = slice_at(buffer, rows, sides[side], -way * (hop - 1))
                source = mine if hop == 1 and side == "own" else target
                send("weights", coming[side, way, hop], source, target, ydev(way))

    def last_weights(side):
        for way in (1, -1):
            arrive(coming[side, way, reach[side, way]], one_slice)

    def block(ref, index):
        return ref.at[pl.ds(index * TOK, TOK)]

    ring = {}

    def pass_meta(hop):
        if hop > 1:
            arrive(ring["m", hop - 1], gm.at[pl.ds(2 * hop - 4, 2)])
        ring["m", hop] = new()
        for way, order in ((1, BEHIND), (-1, AHEAD)):
            if hop > 3 and way < 0:
                continue
            source = gm.at[OWN if hop == 1 else order[hop - 1]]
            send("meta", ring["m", hop], source, gm.at[order[hop]], zdev(way))

    def block_here(name, hop):
        buffer = gx if name == "x" else gc
        arrive(ring[name, hop], buffer.at[pl.ds(2 * (hop - 1) * TOK, TOK if hop == 4 else 2 * TOK)])

    def pass_block(name, hop):
        mine, buffer = {"x": (tok_ref, gx), "c": (cot_ref, gc)}[name]
        if hop > 1:
            block_here(name, hop - 1)
        half = TOK // 2
        ring[name, hop] = new()
        for way, order in ((1, BEHIND), (-1, AHEAD)):
            source = mine if hop == 1 else block(buffer, order[hop - 1])
            target = block(buffer, order[hop])
            if hop == 4:
                part = pl.ds(0 if way > 0 else half, half)
                source, target = source.at[part], target.at[part]
            send("ring", ring[name, hop], source, target, zdev(way))

    pass_block("x", 1)

    ids = ids_ref[...]
    holder = jnp.zeros(ids.shape, F32)
    for e in range(32):
        holder = jnp.where(ids == e, partner_ref[placement_ref[e]].astype(F32), holder)
    gm[OWN, 0:4, :] = holder
    gm[OWN, 4:8, :] = gates_ref[...]
    pass_meta(1)
    pass_block("c", 1)
    across = new()
    for buffer, rows, mine in whole.values():
        send("weights", across, mine, slice_at(buffer, rows, xl, 0), other_side)
    pass_weights("own", 1)
    own_parts = [move(tok_ref, block(gx, OWN)), move(cot_ref, block(gc, OWN))]
    for buffer, rows, mine in whole.values():
        own_parts.append(move(mine, slice_at(buffer, rows, xl, 0)))

    before = lax.broadcasted_iota(jnp.int32, (2 * TOK, 2 * TOK), 0)
    after = lax.broadcasted_iota(jnp.int32, (2 * TOK, 2 * TOK), 1)
    same_block = lax.div(before, TOK) == lax.div(after, TOK)
    tri[...] = jnp.where(same_block & (before < after), 1.0, 0.0).astype(BF16)

    def choose(pair):
        both = jnp.concatenate([gm[2 * pair], gm[2 * pair + 1]], axis=1)
        named, weight = both[0:4], both[4:8]
        hits, scales = [], []
        for q in column:
            hit = jnp.where(named == (z * 4 + q).astype(F32), 1.0, 0.0)
            hits.append(jnp.sum(hit, axis=0, keepdims=True))
            scales.append(jnp.sum(hit * weight, axis=0, keepdims=True))
        marks = jnp.concatenate(hits + [jnp.zeros((12, 2 * TOK), F32)], axis=0)
        ranks = dot(marks.astype(BF16), tri[...], ROWS_COLS)
        slot = lax.broadcasted_iota(jnp.int32, (CAP, 2 * TOK), 0).astype(F32)
        lane = lax.broadcasted_iota(jnp.int32, (CAP, 2 * TOK), 1)
        parts, columns = [], []
        for k in range(4):
            found = (ranks[k : k + 1] == slot) & (hits[k] > 0.5)
            for half in range(2):
                here = lane < TOK if half == 0 else lane >= TOK
                part = jnp.where(found & here, 1.0, 0.0)
                parts.append(part)
                columns.append(jnp.sum(part * scales[k], axis=1, keepdims=True))
        sel[pair] = jnp.concatenate(parts, axis=0).astype(BF16)
        gcol[pair] = jnp.broadcast_to(jnp.concatenate(columns, axis=0), (ROWS, 128))

    there = {}

    def dispatch(name, pair):
        buffer, staged, arrived = {"x": (gx, stx, ex), "c": (gc, stu, eu)}[name]
        for tile in range(0, WIDTH, 512):
            cols = pl.ds(tile, 512)
            rows = dot(sel[pair], buffer[2 * pair * TOK : 2 * (pair + 1) * TOK, cols], ROWS_COLS)
            if name == "c":
                rows = gcol[pair][:, 0:1] * rows
            rows = rows.astype(BF16)
            arrived[pair * ROWS : pair * ROWS + PAIR, cols] = rows[:PAIR]
            staged[pair * 3 * PAIR : (pair + 1) * 3 * PAIR, cols] = rows[PAIR:]
        there[name, pair] = new()
        for k in (2, 3, 1):
            send(
                "out",
                there[name, pair],
                staged.at[pl.ds((pair * 3 + k - 1) * PAIR, PAIR)],
                arrived.at[pl.ds((pair * 4 + k) * PAIR, PAIR)],
                plane[k],
            )

    returned = {}

    def from_others(ref, pair):
        return ref.at[pl.ds(pair * ROWS + PAIR, 3 * PAIR)]

    def rows_here(pair):
        arrive(there["x", pair], from_others(ex, pair))
        arrive(there["c", pair], from_others(eu, pair))

    def expert(pair):
        rows = slice(pair * ROWS, (pair + 1) * ROWS)
        for tile in range(0, FF, 256):
            cols = pl.ds(tile, 256)
            up_cols = pl.ds(FF + tile, 256)
            a = dot(ex[rows], wgu[:, cols], ROWS_COLS)
            b = dot(ex[rows], wgu[:, up_cols], ROWS_COLS)
            dh = dot(eu[rows], wdn[cols], LAST_LAST)
            s = jax.nn.sigmoid(a)
            active = a * s
            hb[rows, cols] = (active * b).astype(BF16)
            qb[rows, cols] = (dh * b * (s * (1.0 + a * (1.0 - s)))).astype(BF16)
            qb[rows, up_cols] = (dh * active).astype(BF16)

    def expert_back(pair):
        rows = slice(pair * ROWS, (pair + 1) * ROWS)
        for tile in range(0, WIDTH, 256):
            cols = pl.ds(tile, 256)
            value = dot(qb[rows], wgu[cols], LAST_LAST).astype(BF16)
            bk[rows, cols] = value
            rb[pair * ROWS : pair * ROWS + PAIR, cols] = value[:PAIR]

    def give_back(pair):
        returned[pair] = new()
        for k in (2, 3, 1):
            part = pl.ds((pair * 4 + k) * PAIR, PAIR)
            send("back", returned[pair], bk.at[part], rb.at[part], plane[k])

    def combine(pair):
        arrive(returned[pair], from_others(rb, pair))
        for tile in range(0, WIDTH, 512):
            cols = pl.ds(tile, 512)
            tgp[pair * 256 : (pair + 1) * 256, cols] = dot(
                sel[pair], rb[pair * ROWS : (pair + 1) * ROWS, cols], FIRST_FIRST
            )

    ways = ((0, 1, BEHIND), (1, -1, AHEAD))
    sums = {}

    def token_step(step, half):
        if step > 1:
            arrive(sums[step - 1, half], rz.at[step - 2, half])
        sums[step, half] = new()
        for index, way, order in ways:
            start, low = order[step] * TOK, index * 512 + half * 256
            term = tgp[start : start + TOK, low : low + 256]
            if step == 1:
                sz[half, index] = term.astype(BF16)
                source = sz.at[half, index]
            else:
                source = rz.at[step - 2, half, index]
                source[...] = (source[...].astype(F32) + term).astype(BF16)
            send("sums", sums[step, half], source, rz.at[step - 1, half, index], zdev(way))

    def token_last():
        for half in range(2):
            arrive(sums[7, half], rz.at[6, half])
            for index, _, _ in ways:
                low = index * 512 + half * 256
                total = tgp[OWN * TOK :, low : low + 256] + rz[6, half, index].astype(F32)
                tg_out[:, low : low + 256] = total.astype(BF16)

    parts = {"dn": (pdn, 0, PARTS[0]), "g0": (pgu, 0, PARTS[1]), "g1": (pgu, 32, PARTS[2])}
    kinds = list(parts)
    both = ("oth", "own")
    chain = {}

    def part_at(kind, side, delta):
        buffer, low, rows = parts[kind]
        return buffer.at[sides[side] * NY + lax.rem(y + delta + NY, NY), pl.ds(low, rows)]

    def grad_here(kind, side, number):
        received = ry[kinds.index(kind)].at[both.index(side), number - 1]
        if number == 4:
            received = received.at[0 if reach[side, 1] == 4 else 1]
        arrive(chain[kind, side, number], received)

    def grad_round(kind, side, number):
        received = ry[kinds.index(kind)].at[both.index(side)]
        if number > 1:
            grad_here(kind, side, number - 1)
        chain[kind, side, number] = new()
        for slot, way in ((0, 1), (1, -1)):
            left = reach[side, way] + 1 - number
            if left < 1:
                continue
            source = part_at(kind, side, way * left)
            if number > 1:
                term = source[...].astype(F32)
                source = received.at[number - 2, slot]
                source[...] = (source[...].astype(F32) + term).astype(BF16)
            target = received.at[number - 1, slot]
            send("grads", chain[kind, side, number], source, target, ydev(way))

    def grad_sum(kind, side):
        grad_here(kind, side, 4)
        total = part_at(kind, side, 0)[...].astype(F32)
        for slot, way in ((0, 1), (1, -1)):
            landed = ry[kinds.index(kind)][both.index(side), reach[side, way] - 1, slot]
            total = total + landed.astype(F32)
        return total

    results = {"dn": (dn_out, 0), "g0": (gu_out, 0), "g1": (gu_out, 32)}
    crossed, moved, spread, reached = {}, {}, {}, {}

    def grad_cross(kind):
        index = kinds.index(kind)
        tx[index][...] = grad_sum(kind, "oth").astype(BF16)
        crossed[kind] = new()
        send("swap", crossed[kind], tx[index], rx[index], other_side)

    def grad_swap(kind):
        index = kinds.index(kind)
        kept, start = results[kind]
        total = grad_sum(kind, "own")
        arrive(crossed[kind], rx[index])
        total = total + rx[index][...].astype(F32)
        kept[start : start + PARTS[index], :] = total
        total = total.astype(BF16)
        sl[index][...] = total
        for piece in range(NZ):
            cut[index][piece] = total[:, piece * 128 : (piece + 1) * 128]
        via[index][0] = cut[index][z]
        spread[kind], moved[kind] = new(), new()
        for r in range(1, NZ):
            source = cut[index].at[lax.rem(z + r, NZ)]
            send("pieces", spread[kind], source, via[index].at[r], zdev(r))
        for bit in (1, 0):
            send("swap", moved[kind], sl[index], rl[index].at[bit], plane[1 << bit])

    def grad_swap_on(kind):
        index = kinds.index(kind)
        arrive(spread[kind], via[index].at[pl.ds(1, NZ - 1)])
        reached[kind] = new()
        for r in range(NZ):
            taker = lax.rem(z + r, NZ)
            giver = lax.div(partner_ref[taker * 4 + c], 4)
            behind = lax.rem(z - giver + NZ, NZ)
            piece = via[index][0]
            for k in range(1, NZ):
                piece = jnp.where(behind == k, via[index][k], piece)
            if r == 0:
                whence[index][z] = piece
                continue
            onward[index][r] = piece
            send("pieces", reached[kind], onward[index].at[r], whence[index].at[z], zdev(r))

    def grad_last(kind):
        index = kinds.index(kind)
        kept, start = results[kind]
        mate = partner_ref[ei]
        arrive(moved[kind], rl[index])
        arrive(reached[kind], whence[index].at[pl.ds(1, NZ - 1)])
        value = kept[start : start + PARTS[index], :]
        for bit in range(2):
            value = jnp.where(mate == flip(ei, bit), rl[index][bit].astype(F32), value)
        pieces = [whence[index][piece].astype(F32) for piece in range(NZ)]
        value = jnp.where(lax.div(mate, 4) == z, value, jnp.concatenate(pieces, axis=1))
        kept[start : start + PARTS[index], :] = value

    early = 3 * ROWS

    def ahead_of_last():
        for tile in range(0, FF, 256):
            cols = pl.ds(tile, 256)
            adn[cols, :] = dot(hb[0:early, cols], eu[0:early], FIRST_FIRST)
        for tile in range(0, WIDTH, 256):
            cols = pl.ds(tile, 256)
            agu[cols, :] = dot(ex[0:early, cols], qb[0:early], FIRST_FIRST)

    def last_dn():
        for tile in range(0, FF, 256):
            cols = pl.ds(tile, 256)
            term = dot(hb[early:, cols], eu[early:], FIRST_FIRST)
            total = (adn[cols, :] + term).astype(BF16)
            pdn[tile // DN : (tile + 256) // DN] = total.reshape(256 // DN, DN, WIDTH)

    def last_gu():
        for tile in range(0, WIDTH, 256):
            cols = pl.ds(tile, 256)
            term = dot(ex[early:, cols], qb[early:], FIRST_FIRST)
            total = (agu[cols, :] + term).astype(BF16)
            pgu[tile // GU : (tile + 256) // GU] = total.reshape(256 // GU, GU, 2 * FF)

    arrive(across, one_slice)
    pass_weights("oth", 1)
    pass_weights("own", 2)
    pass_meta(2)
    pass_block("x", 2)
    choose(0)
    dispatch("x", 0)
    pass_weights("oth", 2)
    pass_block("c", 2)
    dispatch("c", 0)
    pass_weights("own", 3)
    pass_meta(3)
    pass_block("x", 3)
    choose(1)
    dispatch("x", 1)
    pass_weights("oth", 3)
    pass_block("c", 3)
    dispatch("c", 1)
    pass_weights("own", 4)
    pass_weights("oth", 4)
    pass_meta(4)
    pass_block("x", 4)
    choose(2)
    dispatch("x", 2)
    arrive(ring["m", 4], gm.at[OPPOSITE])
    choose(3)
    for copy in own_parts:
        copy.wait()
    pass_block("c", 4)
    dispatch("c", 2)
    last_weights("own")
    last_weights("oth")
    rows_here(0)
    expert(0)
    expert_back(0)
    block_here("x", 4)
    dispatch("x", 3)
    rows_here(1)
    expert(1)
    expert_back(1)
    block_here("c", 4)
    dispatch("c", 3)
    rows_here(2)
    expert(2)
    expert_back(2)
    ahead_of_last()
    rows_here(3)
    give_back(0)
    expert(3)
    last_dn()
    grad_round("dn", "own", 1)
    last_gu()
    grad_round("g0", "oth", 1)
    give_back(1)
    grad_round("g1", "oth", 1)
    grad_round("dn", "oth", 1)
    combine(0)
    grad_round("dn", "own", 2)
    give_back(2)
    token_step(1, 1)
    grad_round("g1", "oth", 2)
    grad_round("g1", "own", 1)
    token_step(1, 0)
    combine(1)
    grad_round("dn", "oth", 2)
    token_step(2, 1)
    grad_round("dn", "own", 3)
    token_step(2, 0)
    grad_round("g0", "own", 1)
    expert_back(3)
    give_back(3)
    combine(2)
    grad_round("dn", "oth", 3)
    grad_round("g1", "own", 2)
    token_step(3, 1)
    token_step(3, 0)
    grad_round("g0", "oth", 2)
    grad_round("g1", "oth", 3)
    grad_round("dn", "oth", 4)
    combine(3)
    token_step(4, 1)
    token_step(4, 0)
    grad_round("g0", "own", 2)
    grad_round("g0", "oth", 3)
    token_step(5, 1)
    grad_round("g1", "own", 3)
    grad_cross("dn")
    grad_round("g1", "oth", 4)
    grad_round("dn", "own", 4)
    token_step(5, 0)
    grad_round("g0", "own", 3)
    token_step(6, 1)
    grad_round("g0", "oth", 4)
    token_step(6, 0)
    grad_swap("dn")
    grad_cross("g1")
    token_step(7, 1)
    grad_round("g1", "own", 4)
    grad_round("g0", "own", 4)
    grad_cross("g0")
    token_step(7, 0)
    grad_swap("g1")
    grad_swap("g0")
    grad_swap_on("dn")
    token_last()
    grad_swap_on("g1")
    grad_swap_on("g0")
    grad_last("dn")
    grad_last("g1")
    grad_last("g0")
    for group, sources in sent.items():
        size = sum(math.prod(source.shape) for source in sources)
        if group == "meta":
            whole_group = gm.at[pl.ds(0, size // (8 * TOK))]
        elif group == "pieces":
            whole_group = hb.at[pl.ds(0, size // FF)]
        else:
            whole_group = agu.at[pl.ds(0, size // (2 * WIDTH))]
        pltpu.make_async_remote_copy(
            src_ref=whole_group,
            dst_ref=whole_group,
            send_sem=ssem.at[GROUPS.index(group)],
            recv_sem=rsem.at[0],
            device_id=other_side,
            device_id_type=MESH,
        ).wait_send()
    assert len(receives) <= RECEIVES


def hand_on(*refs):
    count = len(refs) // 2
    sources, results, sem = refs[:count], refs[count:-1], refs[-1]
    copies = []
    for index in range(count):
        target = results[index] if index == 0 else results[index].at[0]
        copies.append(pltpu.make_async_copy(sources[index], target, sem.at[index]))
        copies[index].start()
    for copy in copies:
        copy.wait()


def body(tokens, cotangent, gates, expert_ids, placement, partner, w_gate_up, w_down):
    def vmem(*shape, dtype=BF16):
        return pltpu.VMEM(shape, dtype)

    slots = 4 * ROWS
    scratch = [
        vmem(NZ * TOK, WIDTH),
        vmem(NZ * TOK, WIDTH),
        vmem(NZ, 8, TOK, dtype=F32),
        vmem(2 * TOK, 2 * TOK),
        vmem(4, ROWS, 2 * TOK),
        vmem(4, ROWS, 128, dtype=F32),
        vmem(12 * PAIR, WIDTH),
        vmem(12 * PAIR, WIDTH),
        vmem(slots, WIDTH),
        vmem(slots, WIDTH),
        vmem(WIDTH, 2 * FF),
        vmem(FF, WIDTH),
        vmem(slots, FF),
        vmem(slots, 2 * FF),
        vmem(slots, WIDTH),
        vmem(slots, WIDTH),
        vmem(NZ * TOK, WIDTH, dtype=F32),
        vmem(2, 2, TOK, 256),
        vmem(7, 2, 2, TOK, 256),
        vmem(WIDTH, 2 * FF, dtype=F32),
        vmem(FF, WIDTH, dtype=F32),
        vmem(16, GU, 2 * FF),
        vmem(16, DN, WIDTH),
        [vmem(2, 4, 2, rows, WIDTH) for rows in PARTS],
        [vmem(rows, WIDTH) for rows in PARTS],
        [vmem(rows, WIDTH) for rows in PARTS],
        [vmem(rows, WIDTH) for rows in PARTS],
        [vmem(2, rows, WIDTH) for rows in PARTS],
        [vmem(NZ, rows, 128) for rows in PARTS],
        [vmem(NZ, rows, 128) for rows in PARTS],
        [vmem(NZ, rows, 128) for rows in PARTS],
        [vmem(NZ, rows, 128) for rows in PARTS],
        pltpu.SemaphoreType.DMA((len(GROUPS),)),
        pltpu.SemaphoreType.DMA((RECEIVES,)),
        pltpu.SemaphoreType.DMA((4,)),
    ]
    in_vmem = pl.BlockSpec(memory_space=pltpu.VMEM)
    in_smem = pl.BlockSpec(memory_space=pltpu.SMEM)
    anywhere = pl.BlockSpec(memory_space=pl.ANY)
    results = pl.pallas_call(
        kernel,
        out_shape=(
            pltpu.VMEM((TOK, WIDTH), BF16),
            pltpu.VMEM((GU, 2 * FF), F32),
            pltpu.VMEM((DN, WIDTH), F32),
        ),
        in_specs=[in_vmem] * 2 + [anywhere] * 4 + [in_smem] * 2,
        out_specs=(in_vmem,) * 3,
        scratch_shapes=scratch,
        compiler_params=pltpu.CompilerParams(
            collective_id=0, has_side_effects=True, vmem_limit_bytes=58 * 1024 * 1024
        ),
    )(expert_ids.T, gates.T, tokens, cotangent, w_gate_up, w_down, placement, partner)
    return pl.pallas_call(
        hand_on,
        out_shape=(
            jax.ShapeDtypeStruct((TOK, WIDTH), BF16),
            jax.ShapeDtypeStruct((1, GU, 2 * FF), F32),
            jax.ShapeDtypeStruct((1, DN, WIDTH), F32),
        ),
        in_specs=[in_vmem] * 3,
        out_specs=(anywhere,) * 3,
        scratch_shapes=[pltpu.SemaphoreType.DMA((3,))],
        compiler_params=pltpu.CompilerParams(vmem_limit_bytes=1024 * 1024),
    )(*results)


def solution(mesh):
    return jax.shard_map(
        body,
        mesh=mesh,
        in_specs=(
            P(("dp", "expert"), None),
            P(("dp", "expert"), None),
            P(("dp", "expert"), None),
            P(("dp", "expert"), None),
            P(),
            P(),
            P("expert", "dp", None),
            P("expert", "dp", None),
        ),
        out_specs=(P(("dp", "expert"), None), P("expert", "dp", None), P("expert", "dp", None)),
        check_vma=False,
    )
```
